256 devices in a mesh: tm: 16 (over x_hi, z), tensor: 16 (over y, x_lo, core).
Axes of the slice: x: 4 (x_hi: 2, x_lo: 2; x = x_hi * 2 + x_lo), y: 4, z: 8, core: 2. Of those that a mesh axis runs over, the one named last changes fastest.
Arguments:
- frames: bfloat16 [16384, 3072], P('tm', 'tensor'), may hold values from -9 to 9
- w_query: bfloat16 [3072, 2048], P(None, 'tensor'), may hold values from -0.09111309 to 0.09111309
- w_key: bfloat16 [3072, 2048], P(None, 'tensor'), may hold values from -0.12719748 to 0.12719748
- w_value: bfloat16 [3072, 2048], P(None, 'tensor'), may hold values from -0.109375 to 0.109375
- w_out: bfloat16 [2048, 3072], P('tensor'), may hold values from -0.125 to 0.125
- head_gain: float32 [3072], P('tensor'), may hold values from 0.25 to 1.75
- reward_weight: float32 [3072, 255], P('tensor'), may hold values from -0.75 to 0.75
- term_weight: float32 [3072], P('tensor'), may hold values from -0.109375 to 0.109375
- out_grad: bfloat16 [16384, 3072], P('tm', 'tensor'), may hold values from -0.75 to 0.75
- reward_bins: int32 [32], P('tm'), may hold values from 0 to 254
- episode_flags: int32 [32], P('tm'), may hold values from 0 to 2
Outputs:
- mixed: bfloat16 [16384, 3072], P('tm', 'tensor')
- pair_losses: float32 [2, 32], P(None, 'tm')
- grad_query: float32 [3072, 2048], P('tm', 'tensor')
- grad_key: float32 [3072, 2048], P('tm', 'tensor')
- grad_value: float32 [3072, 2048], P('tm', 'tensor')
- grad_out: float32 [2048, 3072], P('tensor', 'tm')
- grad_reward: float32 [3072, 255], P('tensor')
- grad_term: float32 [3072], P('tensor')
- grad_gain: float32 [3072], P('tensor')
The draws below stay inside these ranges and needn't reach their ends.
Inputs may be any that keep to these rules, and one draw needn't show every extreme that they name: `episode_flags`: 0: the episode goes on over the pair, 1: it terminates at the pair, 2: the pair straddles a reset and is left out.
All inputs are finite; a program needn't handle non-finite values.
Results may differ from the reference program's by a relative error of at most 0.024.
Values may be sent and summed in bfloat16 or wider, within the bound.
No kernel may reach another device: no remote copies, remote signals or barrier semaphores. Data moves between devices by JAX's collectives and lax.ppermute only.
A program may use at most 128 MiB of HBM per device.

```python
import jax
import jax.numpy as jnp
from jax import lax

D = 3072
HEADS = 16
HD = 128
BINS = 255
PATCHES = 512
FRAMES = 32
ROWS = 16384
N_TENSOR = 16


def shared_query(key):
    normal = jax.random.truncated_normal(jax.random.fold_in(key, 100), -5.0, 5.0, (D, HEADS * HD), jnp.float32)
    return normal * D ** (-0.5)


def draw_w_query(key, part):
    common = shared_query(key)
    return common.astype(jnp.bfloat16)


def draw_w_key(key, part):
    key = jax.random.fold_in(key, 2)
    own = jax.random.truncated_normal(key, -5.0, 5.0, (D, HEADS * HD), jnp.float32) * D ** (-0.5)
    mixed_draw = own
    return mixed_draw.astype(jnp.bfloat16)


def draw_frames(key, part):
    key = jax.random.fold_in(key, 3)
    first = jax.random.fold_in(key, 0)
    values = jax.random.truncated_normal(first, -6.0, 6.0, (ROWS, D), jnp.float32)
    return values.astype(jnp.bfloat16)


def touch_ends(entries, key, low, largest):
    longest = entries.shape.index(max(entries.shape))
    spots = []
    for shift in (0, 1):
        where = [jax.random.randint(jax.random.fold_in(key, axis), (), 0, length) for axis, length in enumerate(entries.shape)]
        where[longest] = (where[longest] + shift) % entries.shape[longest]
        spots.append(tuple(where))
    return entries.at[spots[0]].set(low).at[spots[1]].set(largest)


def levels(rng, extent, shards, smallest, top_value):
    def one(dim, shards_of):
        steps = jax.random.uniform(jax.random.fold_in(jax.random.fold_in(rng, 6), dim), (shards_of,), jnp.float32, smallest / len(shards), top_value / len(shards))
        return jnp.repeat(jnp.exp(steps), extent[dim] // shards_of).reshape((-1,) + (1,) * (len(extent) - dim - 1))

    level = one(*shards[0])
    for cut in shards[1:]:
        level = level * one(*cut)
    return level


def gaussian(own_key, dims, deviation, bound, pieces=(), held_as=jnp.bfloat16):
    drawn = jax.random.normal(own_key, dims, jnp.float32) * deviation
    if len(pieces) > 0:
        drawn = levels(own_key, dims, pieces, -0.22, 0.18) * drawn
    return jnp.clip(drawn, min=-bound, max=bound).astype(held_as)


def setup_inputs(seed: int = 0) -> dict:
    seeds = jax.random.split(jax.random.key(seed), 12)
    frames = draw_frames(jax.random.fold_in(seeds[11], 71), 0)
    w_query = draw_w_query(jax.random.fold_in(seeds[11], 71), 0)
    w_key = draw_w_key(jax.random.fold_in(seeds[11], 71), 0)
    w_value = gaussian(seeds[3], (D, HEADS * HD), D ** -0.5, 0.109375, ((1, 16),))
    w_out = gaussian(seeds[4], (HEADS * HD, D), (HEADS * HD) ** -0.5, 0.125, ((0, 16),))
    head_gain = jnp.clip(1.0 + 0.15 * jax.random.normal(seeds[5], (D,), jnp.float32), 0.25, 1.75)
    reward_weight = gaussian(seeds[6], (D, BINS), (3.0 * D ** -0.5), 0.75, ((0, 16),), jnp.float32)
    term_weight = gaussian(seeds[7], (D,), D ** -0.5, 0.109375, ((0, 16),), jnp.float32)
    out_grad = gaussian(seeds[8], (ROWS, D), 0.05, 0.75, ((0, 16), (1, 16)))
    reward_bins = touch_ends(jax.random.randint(seeds[9], (FRAMES,), 0, BINS), jax.random.fold_in(seeds[9], 1), 0, BINS - 1).astype(jnp.int32)
    episode_flags = touch_ends(jax.random.randint(seeds[10], (FRAMES,), 0, 3), jax.random.fold_in(seeds[10], 1), 0, 2).astype(jnp.int32)
    return {"frames": frames, "w_query": w_query, "w_key": w_key, "w_value": w_value, "w_out": w_out, "head_gain": head_gain, "reward_weight": reward_weight, "term_weight": term_weight, "out_grad": out_grad, "reward_bins": reward_bins, "episode_flags": episode_flags}


def reference(frames, w_query, w_key, w_value, w_out, head_gain, reward_weight, term_weight, out_grad, reward_bins, episode_flags):
    f32 = jnp.float32
    bf16 = jnp.bfloat16
    highest = lax.Precision.HIGHEST
    width = HEADS * HD
    scale_qk = HD ** (-0.5)
    queries = jnp.dot(frames, w_query, preferred_element_type=f32).astype(bf16)
    keys = jnp.dot(frames, w_key, preferred_element_type=f32).astype(bf16)
    values = jnp.dot(frames, w_value, preferred_element_type=f32).astype(bf16)
    keys_pad = jnp.concatenate([keys, jnp.zeros((PATCHES, width), bf16)], 0)
    values_pad = jnp.concatenate([values, jnp.zeros((PATCHES, width), bf16)], 0)
    frames_pad = jnp.concatenate([frames, jnp.zeros((PATCHES, D), bf16)], 0)
    key_index = jnp.arange(2 * PATCHES, dtype=jnp.int32)

    def pair_probs(step):
        start = (step * PATCHES).astype(jnp.int32)
        query_rows = lax.dynamic_slice_in_dim(queries, start, PATCHES, 0).reshape(PATCHES, HEADS, HD)
        key_rows = lax.dynamic_slice_in_dim(keys_pad, start, 2 * PATCHES, 0).reshape(2 * PATCHES, HEADS, HD)
        value_rows = lax.dynamic_slice_in_dim(values_pad, start, 2 * PATCHES, 0).reshape(2 * PATCHES, HEADS, HD)
        scores = jnp.einsum('qhd,khd->hqk', query_rows.astype(f32), key_rows.astype(f32)) * scale_qk
        cut = (step == FRAMES - 1) & (key_index >= PATCHES)
        scores = jnp.where(cut[None, None, :], -1e+30, scores)
        probs = jax.nn.softmax(scores, axis=-1)
        return (query_rows, key_rows, value_rows, probs, start)

    def forward_pair(step):
        query_rows, key_rows, value_rows, probs, start = pair_probs(step)
        weights = probs.astype(bf16)
        out = jnp.einsum('hqk,khd->qhd', weights.astype(f32), value_rows.astype(f32))
        return out.astype(bf16).reshape(PATCHES, width)
    attended = lax.map(forward_pair, jnp.arange(FRAMES, dtype=jnp.int32)).reshape(ROWS, width)
    group = width // N_TENSOR

    def add_group(total, index):
        start = (index * group).astype(jnp.int32)
        cols = lax.dynamic_slice_in_dim(attended, start, group, 1)
        rows_w = lax.dynamic_slice_in_dim(w_out, start, group, 0)
        part = jnp.dot(cols, rows_w, preferred_element_type=f32).astype(bf16)
        return (total + lax.optimization_barrier(part).astype(f32), None)
    summed, _ = lax.scan(add_group, jnp.zeros((ROWS, D), f32), jnp.arange(N_TENSOR, dtype=jnp.int32))
    mixed = (frames.astype(f32) + summed).astype(bf16)
    pooled = mixed.astype(f32).reshape(FRAMES, PATCHES, D).mean(axis=1)
    scale = lax.rsqrt(lax.optimization_barrier(jnp.mean(pooled * pooled, axis=-1, keepdims=True)) + 1e-05)
    gained = pooled * head_gain[None, :]
    reward_logits = scale * jnp.dot(gained, reward_weight, precision=highest)
    term_logit = scale[:, 0] * jnp.dot(gained, term_weight, precision=highest)
    frame_ids = jnp.arange(FRAMES, dtype=jnp.int32)
    live = ((episode_flags != 2) & (frame_ids < FRAMES - 1)).astype(f32)
    target = (episode_flags == 1).astype(f32)
    onehot = (reward_bins[:, None] == jnp.arange(BINS, dtype=jnp.int32)[None, :]).astype(f32)
    reward_loss = live * (jax.scipy.special.logsumexp(reward_logits, axis=-1) - lax.optimization_barrier(jnp.sum(onehot * reward_logits, axis=-1)))
    term_loss = live * (jax.nn.softplus(term_logit) - target * term_logit)
    pair_losses = jnp.stack([reward_loss, term_loss])
    logit_grad = live[:, None] * (jax.nn.softmax(reward_logits, axis=-1) - onehot)
    term_grad = live * (jax.nn.sigmoid(term_logit) - target)
    scale_grad = (lax.optimization_barrier(jnp.sum(logit_grad * reward_logits, axis=-1)) + term_grad * term_logit) / scale[:, 0]
    gain_input_grad = scale * (jnp.dot(logit_grad, reward_weight.T, precision=highest) + term_grad[:, None] * term_weight[None, :])
    pooled_grad = head_gain[None, :] * gain_input_grad - scale_grad[:, None] * scale ** 3 * pooled / D
    grad_reward = jnp.dot(gained.T, scale * logit_grad, precision=highest)
    grad_term = jnp.dot(gained.T, scale[:, 0] * term_grad, precision=highest)
    grad_gain = lax.optimization_barrier(jnp.sum(pooled * gain_input_grad, axis=0))
    mixed_grad = (out_grad.astype(f32).reshape(FRAMES, PATCHES, D) + pooled_grad[:, None, :] / PATCHES).reshape(ROWS, D).astype(bf16)
    grad_out = jnp.dot(attended.T, mixed_grad, preferred_element_type=f32)
    attended_grad = jnp.dot(mixed_grad, w_out.T, preferred_element_type=f32).astype(bf16)

    def backward_pair(carry, step):
        grad_k, grad_v = carry
        query_rows, key_rows, value_rows, probs, start = pair_probs(step)
        weights = probs.astype(bf16)
        out_rows = lax.dynamic_slice_in_dim(attended_grad, start, PATCHES, 0).reshape(PATCHES, HEADS, HD)
        prob_grad = jnp.einsum('qhd,khd->hqk', out_rows.astype(f32), value_rows.astype(f32))
        value_pair = jnp.einsum('hqk,qhd->khd', weights.astype(f32), out_rows.astype(f32)).astype(bf16)
        delta = lax.optimization_barrier(jnp.sum(prob_grad * probs, axis=-1, keepdims=True))
        score_grad = (probs * (prob_grad - delta) * scale_qk).astype(bf16)
        query_grad = jnp.einsum('hqk,khd->qhd', score_grad.astype(f32), key_rows.astype(f32)).astype(bf16)
        key_pair = jnp.einsum('hqk,qhd->khd', score_grad.astype(f32), query_rows.astype(f32)).astype(bf16)
        key_feats = lax.dynamic_slice_in_dim(frames_pad, start, 2 * PATCHES, 0)
        grad_k = grad_k + jnp.dot(key_feats.T, key_pair.reshape(2 * PATCHES, width), preferred_element_type=f32)
        grad_v = grad_v + jnp.dot(key_feats.T, value_pair.reshape(2 * PATCHES, width), preferred_element_type=f32)
        return ((grad_k, grad_v), query_grad.reshape(PATCHES, width))
    start_grads = (jnp.zeros((D, width), f32), jnp.zeros((D, width), f32))
    (grad_key, grad_value), query_grads = lax.scan(backward_pair, start_grads, jnp.arange(FRAMES, dtype=jnp.int32))
    grad_query = jnp.dot(frames.T, query_grads.reshape(ROWS, width), preferred_element_type=f32)
    return (mixed, pair_losses, grad_query, grad_key, grad_value, grad_out, grad_reward, grad_term, grad_gain)
```

```python
import functools

import jax
import jax.numpy as jnp
from jax import lax
from jax.experimental import pallas as pl
from jax.experimental.pallas import tpu as pltpu
from jax.sharding import PartitionSpec as P

HD = 128
PATCHES = 512
NY, NX, NC = 4, 2, 2
NH, NZ = 2, 8
F32 = jnp.float32
BF16 = jnp.bfloat16
VMEM = pl.BlockSpec(memory_space=pltpu.VMEM)
SMEM = pl.BlockSpec(memory_space=pltpu.SMEM)
LOG2E = 1.4426950408889634


def dot(a, b, ca, cb):
    return lax.dot_general(a, b, (((ca,), (cb,)), ((), ())), preferred_element_type=F32)


def split_dot(a, b, ca, cb):
    high = a.astype(BF16)
    low = (a - high.astype(F32)).astype(BF16)
    return dot(high, b, ca, cb) + dot(low, b, ca, cb)


def tensor_permute(x, move):
    pairs = []
    for y in range(NY):
        for h in range(NX):
            for c in range(NC):
                y2, h2, c2 = move(y, h, c)
                pairs.append(((y * NX + h) * NC + c, (y2 * NX + h2) * NC + c2))
    return lax.ppermute(x, "tensor", pairs)


def tm_permute(x, move):
    pairs = []
    for h in range(NH):
        for z in range(NZ):
            h2, z2 = move(h, z)
            pairs.append((h * NZ + z, h2 * NZ + z2))
    return lax.ppermute(x, "tm", pairs)


def from_behind(x, by):
    size = NH * NZ
    pairs = [(i, i + by) for i in range(size) if 0 <= i + by < size]
    return lax.ppermute(x, "tm", pairs)


def sum_over_tensor(x):
    x = x + tensor_permute(x, lambda y, h, c: (y, h, c ^ 1))
    if NX == 2:
        x = x + tensor_permute(x, lambda y, h, c: (y, h ^ 1, c))
    if NY >= 2:
        x = x + tensor_permute(x, lambda y, h, c: (y ^ 1, h, c))
    if NY == 4:
        x = x + tensor_permute(x, lambda y, h, c: (3 - y, h, c))
    return x


def gather_over_tm(x, position):
    def grow(x, bit, move):
        other = tm_permute(x, move)
        low = (position & bit) == 0
        return jnp.concatenate([jnp.where(low, x, other), jnp.where(low, other, x)], 0)

    bit = 1
    while bit < NZ:
        x = grow(x, bit, lambda h, z, bit=bit: (h, z ^ bit))
        bit *= 2
    return grow(x, NZ, lambda h, z: (h ^ 1, z))


def scatter_over_tm(block, position):
    z = lax.rem(position, NZ)
    upper = position >= NZ
    half = NZ // 2

    def right(x):
        return tm_permute(x, lambda h, z: (h, (z + 1) % NZ))

    def left(x):
        return tm_permute(x, lambda h, z: (h, (z - 1) % NZ))

    far = block(lax.rem(z + half, NZ)).astype(BF16)
    r, l = right(far[0]), left(far[1])
    total = None
    for distance in range(half - 1, -1, -1):
        r_block = block(lax.rem(z + distance, NZ))
        l_block = block(lax.rem(z + NZ - distance, NZ)) if distance else 0.0
        if distance == half - 1:
            r_sum = jnp.stack([r_block[0] + r.astype(F32), r_block[1]])
            if distance:
                l_sum = jnp.stack([l_block[0], l_block[1] + l.astype(F32)])
            else:
                total = jnp.stack([r_block[0] + r.astype(F32), r_block[1] + l.astype(F32)])
        elif distance:
            r_sum, l_sum = r_block + r.astype(F32), l_block + l.astype(F32)
        else:
            total = r_block + r.astype(F32) + l.astype(F32)
        if distance:
            r, l = right(r_sum.astype(BF16)), left(l_sum.astype(BF16))
    mine = jnp.where(upper, total[1], total[0])
    theirs = jnp.where(upper, total[0], total[1]).astype(BF16)
    return mine + tm_permute(theirs, lambda h, z: (h ^ 1, z)).astype(F32)


def forward_kernel(pair, q_ref, ka_ref, kb_ref, va_ref, vb_ref, *rest):
    if pair:
        last_ref, first_ref, w_ref, o_ref, p_ref, mean_ref, part_ref = rest
    else:
        o_ref, p_ref = rest
    span = PATCHES
    step = 256
    k_rows = jnp.concatenate([ka_ref[...], kb_ref[...]], 1).T
    v_cols = jnp.concatenate([va_ref[...], vb_ref[...]], 1)
    for at in range(0, span, step):
        s = dot(k_rows, q_ref[:, at : at + step], 1, 0) * (HD ** (-0.5) * LOG2E)
        if pair:
            key = lax.broadcasted_iota(jnp.int32, s.shape, 0)
            s = jnp.where((key >= span) & (last_ref[0] == 1), -1e30, s)
        e = jnp.exp2(s - jnp.max(s, axis=0, keepdims=True))
        p = (e * (1.0 / jnp.sum(e, axis=0, keepdims=True))).astype(BF16)
        p_ref[:, at : at + step] = p
        o_ref[:, at : at + step] = dot(v_cols, p, 1, 0).astype(BF16)
    if pair:
        row = lax.broadcasted_iota(jnp.int32, (16, span), 0)
        one = (jnp.where(row == 0, 1.0, 0.0) / span).astype(BF16)
        two = (jnp.where(row == 1, 1.0, 0.0) / span).astype(BF16)
        mean = dot(one, first_ref[...], 1, 1) + dot(two, o_ref[...], 1, 1)
        mean_ref[...] = mean[:2]
        part_ref[...] = split_dot(mean, w_ref[...], 1, 0)[:2]


def heads_kernel(
    bins_ref,
    flags_ref,
    last_ref,
    sum_ref,
    own_ref,
    head_ref,
    w_ref,
    loss_ref,
    logit_ref,
    pooled_grad_ref,
    pooled_ref,
    shift_ref,
    scratch,
):
    scratch[...] = jnp.zeros_like(scratch)
    scratch[0:2, :] = sum_ref[...] + own_ref[...]
    pooled = scratch[...]
    pooled_ref[...] = pooled[:2]
    width = pooled.shape[1]
    scale = lax.rsqrt(jnp.sum(pooled * pooled, axis=1, keepdims=True) / width + 1e-05)
    logits = scale * split_dot(pooled, head_ref[...], 1, 0)
    rows = lax.broadcasted_iota(jnp.int32, (16, 1), 0)
    col = lax.broadcasted_iota(jnp.int32, logits.shape, 1)
    bins = logits.shape[1] - 1

    def pick(ref):
        return jnp.where(rows == 0, ref[0], ref[1])

    flags = pick(flags_ref)
    live = (rows < 2) & (flags != 2) & ((rows != 1) | (last_ref[0] == 0))
    live = jnp.where(live, 1.0, 0.0)
    target = jnp.where(flags == 1, 1.0, 0.0)
    is_bin = col < bins
    onehot = jnp.where(col == pick(bins_ref), 1.0, 0.0)
    top = jnp.max(jnp.where(is_bin, logits, -1e30), axis=1, keepdims=True)
    e = jnp.where(is_bin, jnp.exp(logits - top), 0.0)
    e_sum = jnp.sum(e, axis=1, keepdims=True)
    reward_loss = live * (jnp.log(e_sum) + top - jnp.sum(onehot * logits, axis=1, keepdims=True))
    term = jnp.sum(jnp.where(is_bin, 0.0, logits), axis=1, keepdims=True)
    small = jnp.exp(-jnp.abs(term))
    term_loss = live * (jnp.maximum(term, 0.0) + jnp.log1p(small) - target * term)
    sigmoid = jnp.where(term >= 0.0, 1.0, small) / (1.0 + small)
    grad = live * jnp.where(is_bin, e / e_sum - onehot, sigmoid - target)
    lane = lax.broadcasted_iota(jnp.int32, (16, 128), 1)
    loss_ref[...] = jnp.where(lane == 0, reward_loss, term_loss)[:8]
    scale_grad = jnp.sum(grad * logits, axis=1, keepdims=True) / scale
    through = scale * split_dot(grad, head_ref[...], 1, 1)
    pooled_grad = through - scale_grad * scale**3 * pooled / width
    logit_ref[...] = (scale * grad)[:2]
    pooled_grad_ref[...] = pooled_grad[:2]
    shift = pooled_grad / PATCHES
    high = shift.astype(BF16)
    low = (shift - high.astype(F32)).astype(BF16)
    shift_ref[...] = dot(w_ref[...], high, 1, 1) + dot(w_ref[...], low, 1, 1)


def backward_kernel(pair, q_ref, ka_ref, kb_ref, va_ref, vb_ref, p_ref, g_ref, shift_ref, *rest):
    if pair:
        dq_ref, da_ref, db_ref = rest
    else:
        add_ref, dq_ref, da_ref, db_ref = rest
    span = PATCHES
    step = 256
    k_cols = jnp.concatenate([ka_ref[...], kb_ref[...]], 1)
    v_rows = jnp.concatenate([va_ref[...], vb_ref[...]], 1).T
    lane = lax.broadcasted_iota(jnp.int32, shift_ref.shape, 1)
    shift = jnp.sum(jnp.where(lane == pair, shift_ref[...], 0.0), axis=1, keepdims=True)
    dk = jnp.zeros((HD, 2 * span), F32)
    dv = jnp.zeros((HD, 2 * span), F32)
    for at in range(0, span, step):
        g = (g_ref[:, at : at + step] + shift).astype(BF16)
        p_low = p_ref[:, at : at + step]
        p = p_low.astype(F32)
        dp = dot(v_rows, g, 1, 0)
        dv = dv + dot(g, p_low, 1, 1)
        delta = jnp.sum(p * dp, axis=0, keepdims=True)
        ds = (p * (dp - delta) * HD ** (-0.5)).astype(BF16)
        dq_ref[:, at : at + step] = dot(k_cols, ds, 1, 0).astype(BF16)
        dk = dk + dot(q_ref[:, at : at + step], ds, 1, 1)
    first = jnp.concatenate([dk[:, :span], dv[:, :span]], 0)
    second = jnp.concatenate([dk[:, span:], dv[:, span:]], 0)
    if pair:
        da_ref[...] = first
        db_ref[...] = second.astype(BF16)
    else:
        da_ref[...] = first
        db_ref[...] = (second + add_ref[...]).astype(BF16)


def call(kernel, out_shape, specs, scratch=(), flops=0, bytes_accessed=0):
    return pl.pallas_call(
        kernel,
        out_shape=[jax.ShapeDtypeStruct(*o) for o in out_shape],
        in_specs=specs,
        out_specs=[VMEM] * len(out_shape),
        scratch_shapes=list(scratch),
        compiler_params=pltpu.CompilerParams(vmem_limit_bytes=48 * 1024 * 1024),
        cost_estimate=pl.CostEstimate(flops=flops, bytes_accessed=bytes_accessed, transcendentals=0),
    )


def local(
    frames,
    w_query,
    w_key,
    w_value,
    w_out,
    head_gain,
    reward_weight,
    term_weight,
    out_grad,
    reward_bins,
    episode_flags,
):
    rows, local_width = frames.shape
    span = PATCHES
    full_width = w_out.shape[1]
    n_tensor = lax.axis_size("tensor")
    position = lax.axis_index("tm")
    me = lax.axis_index("tensor")
    is_last = (position == lax.axis_size("tm") - 1).astype(jnp.int32).reshape(1)
    bins = reward_weight.shape[1]

    def gather(x):
        return lax.all_gather(x, "tensor", axis=0, tiled=True)

    frames_t = frames.T
    x = gather(frames_t)
    w_cols = lax.all_to_all(
        w_out.T.reshape(n_tensor, local_width, HD), "tensor", split_axis=0, concat_axis=0
    )
    w_cols = jnp.transpose(w_cols, (1, 0, 2)).reshape(local_width, n_tensor * HD)
    head_local = jnp.concatenate([reward_weight, term_weight[:, None]], 1)
    head_sent = (head_gain[:, None] * head_local).astype(BF16)
    x, head_sent, grad_local = lax.optimization_barrier((x, head_sent, out_grad.T))
    head_full = gather(head_sent)
    head_full, grad_local = lax.optimization_barrier((head_full, grad_local))
    og = gather(grad_local)

    w_kv = jnp.concatenate([w_key, w_value], 1)
    w_qkv = jnp.concatenate([w_query, w_kv], 1)
    kv0 = dot(w_kv, x[:, :span], 0, 0).astype(BF16)
    kv_next = from_behind(kv0, -1)
    q0 = dot(w_query, x[:, :span], 0, 0).astype(BF16)
    qkv1 = dot(w_qkv, x[:, span:], 0, 0).astype(BF16)
    q1, kv1 = qkv1[:HD], qkv1[HD:]
    attention_flops = 2 * 2 * span * 2 * span * HD
    o_shape = ((HD, span), BF16)
    p_shape = ((2 * span, span), BF16)
    o0, p0 = call(
        functools.partial(forward_kernel, 0),
        [o_shape, p_shape],
        [VMEM] * 5,
        flops=attention_flops,
        bytes_accessed=3 << 20,
    )(q0, kv0[:HD], kv1[:HD], kv0[HD:], kv1[HD:])
    o1, p1, att_mean, part = call(
        functools.partial(forward_kernel, 1),
        [o_shape, p_shape, ((2, HD), F32), ((2, full_width), F32)],
        [VMEM] * 5 + [SMEM, VMEM, VMEM],
        flops=attention_flops,
        bytes_accessed=3 << 20,
    )(q1, kv1[:HD], kv_next[:HD], kv1[HD:], kv_next[HD:], is_last, o0, w_out)
    att = jnp.concatenate([o0, o1], 1)
    pooled_sum = sum_over_tensor(part)
    select = (
        jnp.arange(rows, dtype=jnp.int32)[None, :] // span == jnp.arange(2, dtype=jnp.int32)[:, None]
    )
    frame_mean = dot((select / span).astype(BF16), x, 1, 1)
    loss, logit_grad, pooled_grad, pooled, shift = call(
        heads_kernel,
        [
            ((8, 128), F32),
            ((2, bins + 1), F32),
            ((2, full_width), F32),
            ((2, full_width), F32),
            ((HD, 16), F32),
        ],
        [SMEM] * 3 + [VMEM] * 4,
        [pltpu.VMEM((16, full_width), F32)],
        flops=1 << 24,
        bytes_accessed=3 << 20,
    )(reward_bins, episode_flags, is_last, pooled_sum, frame_mean, head_full, w_out)
    pair_losses = loss[:2, :2].T

    att_full = gather(att)
    mixed = (frames.astype(F32) + dot(att_full, w_cols, 0, 1)).astype(BF16)

    g = dot(w_out, og, 1, 0)
    out_grad_part = dot(og, att, 1, 1)
    grad_out_t = (
        out_grad_part
        + pooled_grad[0][:, None] * att_mean[0:1]
        + pooled_grad[1][:, None] * att_mean[1:2]
    ).reshape(NH, NZ, local_width, HD)
    grad_out = scatter_over_tm(
        lambda i: lax.dynamic_index_in_dim(grad_out_t, i, 1, keepdims=False), position
    ).T

    def backward(pair, q, ka, kb, va, vb, p, g, *add):
        return call(
            functools.partial(backward_kernel, pair),
            [o_shape, ((2 * HD, span), F32), ((2 * HD, span), BF16)],
            [VMEM] * (8 + len(add)),
            flops=attention_flops * 5 // 2,
            bytes_accessed=4 << 20,
        )(q, ka, kb, va, vb, p, g, shift, *add)

    dq1, d_first1, d_next = backward(
        1, q1, kv1[:HD], kv_next[:HD], kv1[HD:], kv_next[HD:], p1, g[:, span:]
    )
    returned = from_behind(d_next, 1)
    dq0, d_first0, d1 = backward(
        0, q0, kv0[:HD], kv1[:HD], kv0[HD:], kv1[HD:], p0, g[:, :span], d_first1
    )
    d0 = (d_first0 + returned.astype(F32)).astype(BF16)
    d_all = jnp.concatenate(
        [jnp.concatenate([dq0, d0], 0), jnp.concatenate([dq1, d1], 0)], 1
    )
    x_blocks = x.reshape(NH, NZ, local_width, rows)

    def block(i):
        return lax.dot_general(
            lax.dynamic_index_in_dim(x_blocks, i, 1, keepdims=False),
            d_all,
            (((2,), (1,)), ((), ())),
            preferred_element_type=F32,
        )

    grads = scatter_over_tm(block, position)
    grad_query, grad_key, grad_value = grads[:, :HD], grads[:, HD : 2 * HD], grads[:, 2 * HD :]

    def mine(a):
        return lax.dynamic_slice_in_dim(a, me * local_width, local_width, 1)

    pooled_mine = mine(pooled)
    gained = pooled_mine * head_gain[None, :]
    gain_in = jnp.dot(logit_grad, head_local.T, precision=lax.Precision.HIGHEST)
    gain_part = jnp.sum(pooled_mine * gain_in, axis=0, keepdims=True)
    small = jnp.concatenate([gained, gain_part], 0)
    small = jnp.pad(small, ((0, 0), (0, bins + 1 - local_width)))
    packed = jnp.concatenate([small, logit_grad, jnp.zeros((3, bins + 1), F32)], 0)
    packed = gather_over_tm(packed, position).reshape(-1, 8, bins + 1)
    gained_all = packed[:, :2, :local_width].reshape(-1, local_width)
    logit_all = packed[:, 3:5].reshape(-1, bins + 1)
    head_grad = lax.dot_general(
        gained_all,
        logit_all,
        (((0,), (0,)), ((), ())),
        precision=lax.Precision.HIGHEST,
        preferred_element_type=F32,
    )
    grad_gain = jnp.sum(packed[:, 2, :local_width], axis=0)
    return (
        mixed,
        pair_losses,
        grad_query,
        grad_key,
        grad_value,
        grad_out,
        head_grad[:, :bins],
        head_grad[:, bins],
        grad_gain,
    )


def solution(mesh):
    return jax.shard_map(
        local,
        mesh=mesh,
        in_specs=(
            P("tm", "tensor"),
            P(None, "tensor"),
            P(None, "tensor"),
            P(None, "tensor"),
            P("tensor", None),
            P("tensor"),
            P("tensor", None),
            P("tensor"),
            P("tm", "tensor"),
            P("tm"),
            P("tm"),
        ),
        out_specs=(
            P("tm", "tensor"),
            P(None, "tm"),
            P("tm", "tensor"),
            P("tm", "tensor"),
            P("tm", "tensor"),
            P("tensor", "tm"),
            P("tensor", None),
            P("tensor"),
            P("tensor"),
        ),
        check_vma=False,
    )
```

```python
import functools

import jax
import jax.numpy as jnp
from jax import lax
from jax.experimental import pallas as pl
from jax.experimental.pallas import tpu as pltpu
from jax.sharding import PartitionSpec as P

HD = 128
PATCHES = 512
NY, NX, NC = 4, 2, 2
NH, NZ = 2, 8
F32 = jnp.float32
BF16 = jnp.bfloat16
VMEM = pl.BlockSpec(memory_space=pltpu.VMEM)
SMEM = pl.BlockSpec(memory_space=pltpu.SMEM)
LOG2E = 1.4426950408889634


def dot(a, b, ca, cb):
    return lax.dot_general(a, b, (((ca,), (cb,)), ((), ())), preferred_element_type=F32)


def split_dot(a, b, ca, cb):
    high = a.astype(BF16)
    low = (a - high.astype(F32)).astype(BF16)
    return dot(high, b, ca, cb) + dot(low, b, ca, cb)


def tensor_permute(x, move):
    pairs = []
    for y in range(NY):
        for h in range(NX):
            for c in range(NC):
                y2, h2, c2 = move(y, h, c)
                pairs.append(((y * NX + h) * NC + c, (y2 * NX + h2) * NC + c2))
    return lax.ppermute(x, "tensor", pairs)


def tm_permute(x, move):
    pairs = []
    for h in range(NH):
        for z in range(NZ):
            h2, z2 = move(h, z)
            pairs.append((h * NZ + z, h2 * NZ + z2))
    return lax.ppermute(x, "tm", pairs)


def from_behind(x, by):
    size = NH * NZ
    pairs = [(i, i + by) for i in range(size) if 0 <= i + by < size]
    return lax.ppermute(x, "tm", pairs)


def sum_over_tensor(x):
    x = x + tensor_permute(x, lambda y, h, c: (y, h, c ^ 1))
    if NX == 2:
        x = x + tensor_permute(x, lambda y, h, c: (y, h ^ 1, c))
    if NY >= 2:
        x = x + tensor_permute(x, lambda y, h, c: (y ^ 1, h, c))
    if NY == 4:
        x = x + tensor_permute(x, lambda y, h, c: (3 - y, h, c))
    return x


def slot_owner(me, slot):
    core, y, x = slot // (NY * NX), slot // NX % NY, slot % NX
    my_y, my_x, my_core = me // (NX * NC), me // NC % NX, me % NC
    return (lax.rem(my_y + y, NY) * NX + (my_x ^ x)) * NC + (my_core ^ core)


def gather_hierarchical(parts):
    n = parts[0].shape[0]
    half = n // 2

    def up(x):
        return tensor_permute(x, lambda y, h, c: ((y + 1) % NY, h, c))

    def down(x):
        return tensor_permute(x, lambda y, h, c: ((y - 1) % NY, h, c))

    def across(x):
        return tensor_permute(x, lambda y, h, c: (y, h ^ 1, c))

    def swap(x):
        return tensor_permute(x, lambda y, h, c: (y, h, c ^ 1))

    results = []
    for part in parts:
        pair, below, above = across(part), up(part), down(part)
        a = up(jnp.concatenate([pair, below[:half]], 0))
        b = down(jnp.concatenate([pair, above[half:]], 0))
        far_a, far_b = up(a[:half]), down(b[half:n])
        own = jnp.concatenate(
            [part, pair, above, b[:n], a[n:], b[n:], far_a, far_b, below, a[:n]], 0
        )
        results.append((own.reshape(NY * NX, n, -1), swap(own).reshape(NY * NX, n, -1)))
    return results


def gather_over_tm(x, position):
    def grow(x, bit, move):
        other = tm_permute(x, move)
        low = (position & bit) == 0
        return jnp.concatenate([jnp.where(low, x, other), jnp.where(low, other, x)], 0)

    bit = 1
    while bit < NZ:
        x = grow(x, bit, lambda h, z, bit=bit: (h, z ^ bit))
        bit *= 2
    return grow(x, NZ, lambda h, z: (h ^ 1, z))


def scatter_over_tm(blocks, position):
    z = lax.rem(position, NZ)
    upper = position >= NZ
    half = NZ // 2

    def block(i):
        return lax.dynamic_index_in_dim(blocks, lax.rem(i, NZ), 1, keepdims=False)

    def right(x):
        return tm_permute(x, lambda h, z: (h, (z + 1) % NZ))

    def left(x):
        return tm_permute(x, lambda h, z: (h, (z - 1) % NZ))

    far = block(z + half)
    r, l = right(far[0]), left(far[1])
    for distance in range(half - 1, 0, -1):
        r_block, l_block = block(z + distance).astype(F32), block(z + NZ - distance).astype(F32)
        if distance == half - 1:
            r_block = jnp.stack([r_block[0] + r.astype(F32), r_block[1]])
            l_block = jnp.stack([l_block[0], l_block[1] + l.astype(F32)])
        else:
            r_block, l_block = r_block + r.astype(F32), l_block + l.astype(F32)
        r, l = right(r_block.astype(BF16)), left(l_block.astype(BF16))
    total = block(z).astype(F32) + r.astype(F32) + l.astype(F32)
    mine = jnp.where(upper, total[1], total[0])
    theirs = jnp.where(upper, total[0], total[1]).astype(BF16)
    return mine + tm_permute(theirs, lambda h, z: (h ^ 1, z)).astype(F32)


def forward_kernel(pair, q_ref, ka_ref, kb_ref, va_ref, vb_ref, *rest):
    if pair:
        last_ref, first_ref, w_ref, o_ref, p_ref, mean_ref, part_ref = rest
    else:
        o_ref, p_ref = rest
    span = PATCHES
    step = 256
    k_rows = jnp.concatenate([ka_ref[...], kb_ref[...]], 1).T
    v_cols = jnp.concatenate([va_ref[...], vb_ref[...]], 1)
    for at in range(0, span, step):
        s = dot(k_rows, q_ref[:, at : at + step], 1, 0) * (HD ** (-0.5) * LOG2E)
        if pair:
            key = lax.broadcasted_iota(jnp.int32, s.shape, 0)
            s = jnp.where((key >= span) & (last_ref[0] == 1), -1e30, s)
        e = jnp.exp2(s - jnp.max(s, axis=0, keepdims=True))
        p = (e * (1.0 / jnp.sum(e, axis=0, keepdims=True))).astype(BF16)
        p_ref[:, at : at + step] = p
        o_ref[:, at : at + step] = dot(v_cols, p, 1, 0).astype(BF16)
    if pair:
        row = lax.broadcasted_iota(jnp.int32, (16, span), 0)
        one = (jnp.where(row == 0, 1.0, 0.0) / span).astype(BF16)
        two = (jnp.where(row == 1, 1.0, 0.0) / span).astype(BF16)
        mean = dot(one, first_ref[...], 1, 1) + dot(two, o_ref[...], 1, 1)
        mean_ref[...] = mean[:2]
        part_ref[...] = split_dot(mean, w_ref[...], 1, 0)[:2]


def heads_kernel(
    bins_ref,
    flags_ref,
    last_ref,
    sum_ref,
    head_ref,
    w_ref,
    loss_ref,
    logit_ref,
    pooled_grad_ref,
    pooled_ref,
    shift_ref,
    scratch,
):
    scratch[...] = jnp.zeros_like(scratch)
    scratch[0:2, :] = sum_ref[...]
    pooled = scratch[...]
    pooled_ref[...] = pooled[:2]
    width = pooled.shape[1]
    scale = lax.rsqrt(jnp.sum(pooled * pooled, axis=1, keepdims=True) / width + 1e-05)
    logits = scale * split_dot(pooled, head_ref[...], 1, 0)
    rows = lax.broadcasted_iota(jnp.int32, (16, 1), 0)
    col = lax.broadcasted_iota(jnp.int32, logits.shape, 1)
    bins = logits.shape[1] - 1

    def pick(ref):
        return jnp.where(rows == 0, ref[0], ref[1])

    flags = pick(flags_ref)
    live = (rows < 2) & (flags != 2) & ((rows != 1) | (last_ref[0] == 0))
    live = jnp.where(live, 1.0, 0.0)
    target = jnp.where(flags == 1, 1.0, 0.0)
    is_bin = col < bins
    onehot = jnp.where(col == pick(bins_ref), 1.0, 0.0)
    top = jnp.max(jnp.where(is_bin, logits, -1e30), axis=1, keepdims=True)
    e = jnp.where(is_bin, jnp.exp(logits - top), 0.0)
    e_sum = jnp.sum(e, axis=1, keepdims=True)
    reward_loss = live * (jnp.log(e_sum) + top - jnp.sum(onehot * logits, axis=1, keepdims=True))
    term = jnp.sum(jnp.where(is_bin, 0.0, logits), axis=1, keepdims=True)
    small = jnp.exp(-jnp.abs(term))
    term_loss = live * (jnp.maximum(term, 0.0) + jnp.log1p(small) - target * term)
    sigmoid = jnp.where(term >= 0.0, 1.0, small) / (1.0 + small)
    grad = live * jnp.where(is_bin, e / e_sum - onehot, sigmoid - target)
    lane = lax.broadcasted_iota(jnp.int32, (16, 128), 1)
    loss_ref[...] = jnp.where(lane == 0, reward_loss, term_loss)[:8]
    scale_grad = jnp.sum(grad * logits, axis=1, keepdims=True) / scale
    through = scale * split_dot(grad, head_ref[...], 1, 1)
    pooled_grad = through - scale_grad * scale**3 * pooled / width
    logit_ref[...] = (scale * grad)[:2]
    pooled_grad_ref[...] = pooled_grad[:2]
    shift = pooled_grad / PATCHES
    high = shift.astype(BF16)
    low = (shift - high.astype(F32)).astype(BF16)
    shift_ref[...] = dot(w_ref[...], high, 1, 1) + dot(w_ref[...], low, 1, 1)


def backward_kernel(pair, q_ref, ka_ref, kb_ref, va_ref, vb_ref, p_ref, g_ref, shift_ref, *rest):
    if pair:
        dq_ref, da_ref, db_ref = rest
    else:
        add_ref, dq_ref, da_ref, db_ref = rest
    span = PATCHES
    step = 256
    k_cols = jnp.concatenate([ka_ref[...], kb_ref[...]], 1)
    v_rows = jnp.concatenate([va_ref[...], vb_ref[...]], 1).T
    lane = lax.broadcasted_iota(jnp.int32, shift_ref.shape, 1)
    shift = jnp.sum(jnp.where(lane == pair, shift_ref[...], 0.0), axis=1, keepdims=True)
    dk = jnp.zeros((HD, 2 * span), F32)
    dv = jnp.zeros((HD, 2 * span), F32)
    for at in range(0, span, step):
        g = (g_ref[:, at : at + step] + shift).astype(BF16)
        p_low = p_ref[:, at : at + step]
        p = p_low.astype(F32)
        dp = dot(v_rows, g, 1, 0)
        dv = dv + dot(g, p_low, 1, 1)
        delta = jnp.sum(p * dp, axis=0, keepdims=True)
        ds = (p * (dp - delta) * HD ** (-0.5)).astype(BF16)
        dq_ref[:, at : at + step] = dot(k_cols, ds, 1, 0).astype(BF16)
        dk = dk + dot(q_ref[:, at : at + step], ds, 1, 1)
    first = jnp.concatenate([dk[:, :span], dv[:, :span]], 0)
    second = jnp.concatenate([dk[:, span:], dv[:, span:]], 0)
    if pair:
        da_ref[...] = first
        db_ref[...] = second.astype(BF16)
    else:
        da_ref[...] = first
        db_ref[...] = (second + add_ref[...]).astype(BF16)


def grads_kernel(
    slots_ref,
    own0_ref,
    own1_ref,
    other0_ref,
    other1_ref,
    og_ref,
    pooled_grad_ref,
    dq0_ref,
    d0_ref,
    dq1_ref,
    d1_ref,
    att_ref,
    mean_ref,
    out_ref,
):
    step = pl.program_id(0)

    def fill(x0, x1):
        out_ref[0, :, :HD] = (dot(x0, dq0_ref[...], 1, 1) + dot(x1, dq1_ref[...], 1, 1)).astype(BF16)
        out_ref[0, :, HD : 3 * HD] = (
            dot(x0, d0_ref[...], 1, 1) + dot(x1, d1_ref[...], 1, 1)
        ).astype(BF16)

    @pl.when(step < pl.num_programs(0) // 2)
    def _():
        fill(own0_ref[0], own1_ref[0])

    @pl.when(step >= pl.num_programs(0) // 2)
    def _():
        fill(other0_ref[0], other1_ref[0])

    part = dot(og_ref[0], att_ref[...], 1, 1)
    for pair in range(2):
        part = part + pooled_grad_ref[0, :, pair : pair + 1] * mean_ref[pair : pair + 1, :]
    out_ref[0, :, 3 * HD :] = part.astype(BF16)


def weight_grads(slots, own0, own1, other0, other1, og, pooled_grad, *whole):
    count, n, span = 2 * own0.shape[0], own0.shape[1], own0.shape[2]
    half = count // 2

    def own(s, slots):
        return jnp.minimum(s, half - 1), 0, 0

    def other(s, slots):
        return jnp.maximum(s - half, 0), 0, 0

    def owner(s, slots):
        return slots[s], 0, 0

    return pl.pallas_call(
        grads_kernel,
        grid_spec=pltpu.PrefetchScalarGridSpec(
            num_scalar_prefetch=1,
            grid=(count,),
            in_specs=[
                pl.BlockSpec((1, n, span), own),
                pl.BlockSpec((1, n, span), own),
                pl.BlockSpec((1, n, span), other),
                pl.BlockSpec((1, n, span), other),
                pl.BlockSpec((1, n, 2 * span), owner),
                pl.BlockSpec((1, n, 2), owner),
            ]
            + [VMEM] * len(whole),
            out_specs=pl.BlockSpec((1, n, 4 * HD), owner),
        ),
        out_shape=jax.ShapeDtypeStruct((count, n, 4 * HD), BF16),
        compiler_params=pltpu.CompilerParams(vmem_limit_bytes=48 * 1024 * 1024),
        cost_estimate=pl.CostEstimate(
            flops=2 * count * n * 4 * HD * 2 * span, bytes_accessed=16 << 20, transcendentals=0
        ),
    )(slots, own0, own1, other0, other1, og, pooled_grad, *whole)


def call(kernel, out_shape, specs, scratch=(), flops=0, bytes_accessed=0):
    return pl.pallas_call(
        kernel,
        out_shape=[jax.ShapeDtypeStruct(*o) for o in out_shape],
        in_specs=specs,
        out_specs=[VMEM] * len(out_shape),
        scratch_shapes=list(scratch),
        compiler_params=pltpu.CompilerParams(vmem_limit_bytes=48 * 1024 * 1024),
        cost_estimate=pl.CostEstimate(flops=flops, bytes_accessed=bytes_accessed, transcendentals=0),
    )


def local(
    frames,
    w_query,
    w_key,
    w_value,
    w_out,
    head_gain,
    reward_weight,
    term_weight,
    out_grad,
    reward_bins,
    episode_flags,
):
    rows, local_width = frames.shape
    span = PATCHES
    full_width = w_out.shape[1]
    n_tensor = lax.axis_size("tensor")
    position = lax.axis_index("tm")
    me = lax.axis_index("tensor")
    is_last = (position == lax.axis_size("tm") - 1).astype(jnp.int32).reshape(1)
    bins = reward_weight.shape[1]

    def gather(x):
        return lax.all_gather(x, "tensor", axis=0, tiled=True)

    head_local = jnp.concatenate([reward_weight, term_weight[:, None]], 1)
    head_full = gather((head_gain[:, None] * head_local).astype(BF16))
    frames_t = frames.T
    (own0, other0), (own1, other1) = gather_hierarchical([frames_t[:, :span], frames_t[:, span:]])
    frame_mean = frames.astype(F32).reshape(2, span, local_width).mean(axis=1)
    frame_mean = lax.dynamic_update_slice_in_dim(
        jnp.zeros((2, full_width), F32), frame_mean, me * local_width, 1
    )
    slots = jnp.stack([slot_owner(me, s) for s in range(n_tensor)]).astype(jnp.int32)
    w_qkv = jnp.concatenate([w_query, w_key, w_value], 1).reshape(n_tensor, local_width, 3 * HD)
    half = n_tensor // 2

    def pick(first):
        picked = [
            lax.dynamic_index_in_dim(w_qkv, slots[s], 0) for s in range(first, first + half)
        ]
        return jnp.concatenate(picked, 0).reshape(half * local_width, 3 * HD)

    w_own, w_other = pick(0), pick(half)

    def project(columns, own, other):
        return (
            dot(w_own[:, columns], own.reshape(-1, span), 0, 0)
            + dot(w_other[:, columns], other.reshape(-1, span), 0, 0)
        ).astype(BF16)

    kv0 = project(slice(HD, 3 * HD), own0, other0)
    kv_next = from_behind(kv0, -1)
    q0 = project(slice(0, HD), own0, other0)
    qkv1 = project(slice(0, 3 * HD), own1, other1)
    q1, kv1 = qkv1[:HD], qkv1[HD:]
    grad_local, _ = lax.optimization_barrier((out_grad.T, other1))
    og = gather(grad_local)
    attention_flops = 2 * 2 * span * 2 * span * HD
    o_shape = ((HD, span), BF16)
    p_shape = ((2 * span, span), BF16)
    o0, p0 = call(
        functools.partial(forward_kernel, 0),
        [o_shape, p_shape],
        [VMEM] * 5,
        flops=attention_flops,
        bytes_accessed=3 << 20,
    )(q0, kv0[:HD], kv1[:HD], kv0[HD:], kv1[HD:])
    o1, p1, att_mean, part = call(
        functools.partial(forward_kernel, 1),
        [o_shape, p_shape, ((2, HD), F32), ((2, full_width), F32)],
        [VMEM] * 5 + [SMEM, VMEM, VMEM],
        flops=attention_flops,
        bytes_accessed=3 << 20,
    )(q1, kv1[:HD], kv_next[:HD], kv1[HD:], kv_next[HD:], is_last, o0, w_out)
    att = jnp.concatenate([o0, o1], 1)
    pooled_sum = sum_over_tensor(part + frame_mean)
    loss, logit_grad, pooled_grad, pooled, shift = call(
        heads_kernel,
        [
            ((8, 128), F32),
            ((2, bins + 1), F32),
            ((2, full_width), F32),
            ((2, full_width), F32),
            ((HD, 16), F32),
        ],
        [SMEM] * 3 + [VMEM] * 3,
        [pltpu.VMEM((16, full_width), F32)],
        flops=1 << 24,
        bytes_accessed=3 << 20,
    )(reward_bins, episode_flags, is_last, pooled_sum, head_full, w_out)
    pair_losses = loss[:2, :2].T

    w_send, _ = lax.optimization_barrier((w_out.T, shift))
    w_cols = lax.all_to_all(
        w_send.reshape(n_tensor, local_width, HD), "tensor", split_axis=0, concat_axis=0
    )
    w_cols = jnp.transpose(w_cols, (1, 0, 2)).reshape(local_width, n_tensor * HD)

    g = dot(w_out, og, 1, 0)
    att_sent, g = lax.optimization_barrier((att, g))
    att_full = gather(att_sent)

    def backward(pair, q, ka, kb, va, vb, p, g, *add):
        return call(
            functools.partial(backward_kernel, pair),
            [o_shape, ((2 * HD, span), F32), ((2 * HD, span), BF16)],
            [VMEM] * (8 + len(add)),
            flops=attention_flops * 5 // 2,
            bytes_accessed=4 << 20,
        )(q, ka, kb, va, vb, p, g, shift, *add)

    dq1, d_first1, d_next = backward(
        1, q1, kv1[:HD], kv_next[:HD], kv1[HD:], kv_next[HD:], p1, g[:, span:]
    )
    returned = from_behind(d_next, 1)
    dq0, d_first0, d1 = backward(
        0, q0, kv0[:HD], kv1[:HD], kv0[HD:], kv1[HD:], p0, g[:, :span], d_first1
    )
    d0 = (d_first0 + returned.astype(F32)).astype(BF16)
    blocks = weight_grads(
        slots,
        own0,
        own1,
        other0,
        other1,
        og.reshape(n_tensor, local_width, rows),
        pooled_grad.T.reshape(n_tensor, local_width, 2),
        dq0,
        d0,
        dq1,
        d1,
        att,
        att_mean,
    )
    grads = scatter_over_tm(blocks.reshape(NH, NZ, local_width, 4 * HD), position)
    grad_query, grad_key, grad_value = grads[:, :HD], grads[:, HD : 2 * HD], grads[:, 2 * HD : 3 * HD]
    grad_out = grads[:, 3 * HD :].T

    att_full, _ = lax.optimization_barrier((att_full, blocks))
    mixed = (frames.astype(F32) + dot(att_full, w_cols, 0, 1)).astype(BF16)

    def mine(a):
        return lax.dynamic_slice_in_dim(a, me * local_width, local_width, 1)

    pooled_mine = mine(pooled)
    gained = pooled_mine * head_gain[None, :]
    gain_in = jnp.dot(logit_grad, head_local.T, precision=lax.Precision.HIGHEST)
    gain_part = jnp.sum(pooled_mine * gain_in, axis=0, keepdims=True)
    small = jnp.concatenate([gained, gain_part], 0)
    small = jnp.pad(small, ((0, 0), (0, bins + 1 - local_width)))
    packed = jnp.concatenate([small, logit_grad, jnp.zeros((3, bins + 1), F32)], 0)
    packed = gather_over_tm(packed, position).reshape(-1, 8, bins + 1)
    gained_all = packed[:, :2, :local_width].reshape(-1, local_width)
    logit_all = packed[:, 3:5].reshape(-1, bins + 1)
    head_grad = lax.dot_general(
        gained_all,
        logit_all,
        (((0,), (0,)), ((), ())),
        precision=lax.Precision.HIGHEST,
        preferred_element_type=F32,
    )
    grad_gain = jnp.sum(packed[:, 2, :local_width], axis=0)
    return (
        mixed,
        pair_losses,
        grad_query,
        grad_key,
        grad_value,
        grad_out,
        head_grad[:, :bins],
        head_grad[:, bins],
        grad_gain,
    )


def solution(mesh):
    return jax.shard_map(
        local,
        mesh=mesh,
        in_specs=(
            P("tm", "tensor"),
            P(None, "tensor"),
            P(None, "tensor"),
            P(None, "tensor"),
            P("tensor", None),
            P("tensor"),
            P("tensor", None),
            P("tensor"),
            P("tm", "tensor"),
            P("tm"),
            P("tm"),
        ),
        out_specs=(
            P("tm", "tensor"),
            P(None, "tm"),
            P("tm", "tensor"),
            P("tm", "tensor"),
            P("tm", "tensor"),
            P("tensor", "tm"),
            P("tensor", None),
            P("tensor"),
            P("tensor"),
        ),
        check_vma=False,
    )
```

```python
import functools

import jax
import jax.numpy as jnp
from jax import lax
from jax.experimental import pallas as pl
from jax.experimental.pallas import tpu as pltpu
from jax.sharding import PartitionSpec as P

HD = 128
PATCHES = 512
NY, NX, NC = 4, 2, 2
NH, NZ = 2, 8
F32 = jnp.float32
BF16 = jnp.bfloat16
VMEM = pl.BlockSpec(memory_space=pltpu.VMEM)
SMEM = pl.BlockSpec(memory_space=pltpu.SMEM)
LOG2E = 1.4426950408889634


def dot(a, b, ca, cb):
    return lax.dot_general(a, b, (((ca,), (cb,)), ((), ())), preferred_element_type=F32)


def split_dot(a, b, ca, cb):
    high = a.astype(BF16)
    low = (a - high.astype(F32)).astype(BF16)
    return dot(high, b, ca, cb) + dot(low, b, ca, cb)


def tensor_permute(x, move):
    pairs = []
    for y in range(NY):
        for h in range(NX):
            for c in range(NC):
                y2, h2, c2 = move(y, h, c)
                pairs.append(((y * NX + h) * NC + c, (y2 * NX + h2) * NC + c2))
    return lax.ppermute(x, "tensor", pairs)


def tm_permute(x, move):
    pairs = []
    for h in range(NH):
        for z in range(NZ):
            h2, z2 = move(h, z)
            pairs.append((h * NZ + z, h2 * NZ + z2))
    return lax.ppermute(x, "tm", pairs)


def from_behind(x, by):
    size = NH * NZ
    return lax.ppermute(x, "tm", [(i, (i + by) % size) for i in range(size)])


def sum_over_tensor(x):
    x = x + tensor_permute(x, lambda y, h, c: (y, h, c ^ 1))
    across = tensor_permute(x, lambda y, h, c: (y, h ^ 1, c))
    beside = tensor_permute(x, lambda y, h, c: (y ^ 1, h, c))
    both = tensor_permute(x, lambda y, h, c: (y ^ 1, h ^ 1, c))
    x = (x + across) + (beside + both)
    return x + tensor_permute(x, lambda y, h, c: (3 - y, h, c))


ORDER = ((0, 0), (0, 1), (1, 0), (3, 0), (3, 1), (1, 1), (2, 0), (2, 1))


def slot_owner(me, slot):
    (y, x), core = ORDER[slot // 8 * 4 + slot % 4], slot // 4 % 2
    my_y, my_x, my_core = me // (NX * NC), me // NC % NX, me % NC
    return (lax.rem(my_y + y, NY) * NX + (my_x ^ x)) * NC + (my_core ^ core)


def owner_slot(me, owner):
    y = lax.rem(owner // (NX * NC) + NY - me // (NX * NC), NY)
    x = (owner // NC % NX) ^ (me // NC % NX)
    place = 0
    for i, (its_y, its_x) in enumerate(ORDER):
        place = place + jnp.where((y == its_y) & (x == its_x), i // 4 * 8 + i % 4, 0)
    return place + 4 * ((owner % NC) ^ (me % NC))


def gather_hierarchical(part, beside, use_near):
    def up(x):
        return tensor_permute(x, lambda y, h, c: ((y + 1) % NY, h, c))

    def down(x):
        return tensor_permute(x, lambda y, h, c: ((y - 1) % NY, h, c))

    def across(x):
        return tensor_permute(x, lambda y, h, c: (y, h ^ 1, c))

    def swap(x):
        return tensor_permute(x, lambda y, h, c: (y, h, c ^ 1))

    below, above, pair, part_other = up(part), down(part), across(part), swap(part)
    below, above, pair, part_other, beside = lax.optimization_barrier(
        (below, above, pair, part_other, beside)
    )
    pair_below, pair_above, opposite = up(pair), down(pair), up(below)
    near = (part, pair, above, below, part_other, swap(pair), swap(above), swap(below))
    pair_above, used = lax.optimization_barrier((pair_above, use_near(near, beside)))
    far = (pair_below, pair_above, opposite, down(pair_above))
    return far + tuple(swap(x) for x in far), beside, used


def add_parts(out_ref, row, parts, received=()):
    n = parts[0].shape[1]
    at = 0
    for part in parts:
        columns = slice(at, at + part.shape[2])
        at += part.shape[2]
        total = part[0]
        if received:
            total = total.astype(F32)
            for ref, first in received:
                total = total + ref[first : first + n, columns].astype(F32)
        out_ref[row : row + n, columns] = total.astype(out_ref.dtype)


def ring_first_kernel(count, idx_ref, *refs):
    parts, (*extra, r_ref, l_ref) = refs[: 2 * count], refs[2 * count :]
    n = parts[0].shape[1]
    for h, out_ref in enumerate((r_ref, l_ref)):
        add_parts(out_ref, 0, parts[h * count : (h + 1) * count])
        for ref in extra:
            out_ref[n:, :] = ref[...]


def ring_step_kernel(count, first, idx_ref, r_in, l_in, *refs):
    parts, outs = refs[: 4 * count], refs[4 * count :]
    n = parts[0].shape[1]
    for side, (received, out_ref) in enumerate(zip((r_in, l_in), outs)):
        for h in range(NH):
            block = parts[(2 * side + h) * count : (2 * side + h + 1) * count]
            if first:
                add_parts(out_ref, h * n, block, [(received, 0)] if h == side else [])
            else:
                add_parts(out_ref, h * n, block, [(received, h * n)])
        few = out_ref.shape[0] - 2 * n
        if few:
            extra = received[received.shape[0] - few :, :]
            out_ref[2 * n :, :] = extra
            outs[2 + side][...] = extra


def ring_last_kernel(count, idx_ref, r_in, l_in, *refs):
    parts, (*extras, mine_ref, theirs_ref, scratch) = refs[: 2 * count], refs[2 * count :]
    n = parts[0].shape[1]
    few = extras[0].shape[0] if extras else 0
    extras = [ref[...] for ref in extras]
    if few:
        extras.insert(NZ // 2, r_in[2 * n :, :])
    for h in range(NH):
        block = parts[h * count : (h + 1) * count]
        add_parts(scratch, h * n, block, [(r_in, h * n), (l_in, h * n)])
    upper = idx_ref[0] == 1
    low, high = scratch[:n, :], scratch[n:, :]
    mine_ref[...] = jnp.where(upper, high, low)
    theirs_ref[:n, :] = jnp.where(upper, low, high).astype(BF16)
    z = idx_ref[1]
    shifts = [0] + [-1 - k for k in range(NZ // 2)] + [1 + k for k in range(NZ // 2 - 1)]
    for shift, extra in zip(shifts, extras):
        owner = lax.rem(z + NZ + shift, NZ)
        theirs_ref[pl.ds(pl.multiple_of(n + few * owner, few), few), :] = extra


def ring_indices(position, me):
    z = lax.rem(position, NZ)
    half = NZ // 2
    idx = [(position >= NZ).astype(jnp.int32), z]
    for distance in range(half, -1, -1):
        owners = [
            h * NZ + lax.rem(z + NZ + sign * distance, NZ) for sign in (1, -1) for h in range(NH)
        ]
        idx += [owner_slot(me, owner) for owner in owners] + owners
    return jnp.stack([i.astype(jnp.int32) for i in idx])


class Ring:
    def __init__(self, idx, by_slot, by_owner, extra, position):
        self.idx, self.position = idx, position
        self.arrays = [(x, 0) for x in by_slot] + [(x, 4) for x in by_owner]
        self.n = self.arrays[0][0].shape[1]
        self.columns = sum(x.shape[2] for x, _ in self.arrays)
        self.extras = [] if extra is None else [extra]
        self.few = sum(x.shape[0] for x in self.extras)
        self.rights, self.lefts = [], []

    def blocks(self, step, number):
        def place(which):
            return lambda i, idx: (idx[2 + 8 * step + which], 0, 0)

        specs, args = [], []
        for k in range(number):
            for x, base in self.arrays:
                specs.append(pl.BlockSpec((1,) + x.shape[1:], place(base + k)))
                args.append(x)
        return specs, args

    def run(self, kernel, after, specs, args, out_shape, scratch=()):
        def body(idx_ref, _, *refs):
            kernel(len(self.arrays), idx_ref, *refs)

        return pl.pallas_call(
            body,
            grid_spec=pltpu.PrefetchScalarGridSpec(
                num_scalar_prefetch=1,
                grid=(1,),
                in_specs=[pl.BlockSpec(memory_space=pl.ANY)] + specs,
                out_specs=[VMEM] * len(out_shape),
                scratch_shapes=list(scratch),
            ),
            out_shape=[jax.ShapeDtypeStruct(*o) for o in out_shape],
            compiler_params=pltpu.CompilerParams(vmem_limit_bytes=16 * 1024 * 1024),
            cost_estimate=pl.CostEstimate(flops=5 << 30, bytes_accessed=2 << 20, transcendentals=0),
        )(self.idx, after, *args)

    def send(self):
        self.r = tm_permute(self.r, lambda h, z: (h, (z + 1) % NZ))
        self.l = tm_permute(self.l, lambda h, z: (h, (z - 1) % NZ))

    def first(self, after):
        specs, args = self.blocks(0, 2)
        self.r, self.l = self.run(
            ring_first_kernel,
            after,
            specs + [VMEM] * len(self.extras),
            args + self.extras,
            [((self.n + self.few, self.columns), BF16)] * 2,
        )

    def step(self, step, after):
        specs, args = self.blocks(step, 4)

        def kernel(count, *refs):
            ring_step_kernel(count, step == 1, *refs)

        few = [((self.few, self.columns), BF16)] * 2 if self.few else []
        self.r, self.l, *passed = self.run(
            kernel,
            after,
            [VMEM] * 2 + specs,
            [self.r, self.l] + args,
            [((2 * self.n + self.few, self.columns), BF16)] * 2 + few,
        )
        self.rights += passed[:1]
        self.lefts += passed[1:]

    def last(self, after):
        few, columns = self.few, self.columns
        specs, args = self.blocks(NZ // 2, 2)
        passed = self.rights + self.lefts
        self.mine, self.r = self.run(
            ring_last_kernel,
            after,
            [VMEM] * 2 + specs + [VMEM] * len(self.extras + passed),
            [self.r, self.l] + args + self.extras + passed,
            [((self.n, columns), F32), ((self.n + NZ * few, columns), BF16)],
            [pltpu.VMEM((2 * self.n, columns), F32)],
        )

    def exchange(self):
        return tm_permute(self.r, lambda h, z: (h ^ 1, z))

    def finish(self, other):
        upper = self.position >= NZ
        total = self.mine + other[: self.n].astype(F32)
        if not self.few:
            return total, None
        theirs, other = self.r[self.n :], other[self.n :]
        gathered = [jnp.where(upper, other, theirs), jnp.where(upper, theirs, other)]
        return total, jnp.concatenate(gathered, 0)


def scatter_over_tm(one, two, beside, late):
    half = NZ // 2
    one.first(one.idx)
    two.first(one.r)
    for step in range(1, half + 1):
        before = two.r
        one.send()
        two.send()
        if step < half:
            one.step(step, before)
            two.step(step, one.r)
        else:
            one.last(before)
            two.last(one.r)
    others = one.exchange(), two.exchange()
    others, result = lax.optimization_barrier((others, late(beside)))
    return one.finish(others[0]), two.finish(others[1]), result


def forward_kernel(pair, q_ref, ka_ref, kb_ref, va_ref, vb_ref, *rest):
    if pair:
        last_ref, first_ref, w_ref, o_ref, t_ref, p_ref, mean_ref, part_ref = rest
    else:
        o_ref, t_ref, p_ref = rest
    span = PATCHES
    step = 256
    k_rows = jnp.concatenate([ka_ref[...], kb_ref[...]], 1).T
    v_cols = jnp.concatenate([va_ref[...], vb_ref[...]], 1)
    for at in range(0, span, step):
        s = dot(k_rows, q_ref[:, at : at + step], 1, 0) * (HD ** (-0.5) * LOG2E)
        if pair:
            key = lax.broadcasted_iota(jnp.int32, s.shape, 0)
            s = jnp.where((key >= span) & (last_ref[0] == 1), -1e30, s)
        e = jnp.exp2(s - jnp.max(s, axis=0, keepdims=True))
        p = (e * (1.0 / jnp.sum(e, axis=0, keepdims=True))).astype(BF16)
        p_ref[:, at : at + step] = p
        o = dot(v_cols, p, 1, 0)
        o_ref[:, at : at + step] = o.astype(BF16)
        t_ref[at : at + step, :] = o.T.astype(BF16)
    if pair:
        row = lax.broadcasted_iota(jnp.int32, (16, span), 0)
        one = (jnp.where(row == 0, 1.0, 0.0) / span).astype(BF16)
        two = (jnp.where(row == 1, 1.0, 0.0) / span).astype(BF16)
        mean = dot(one, first_ref[...], 1, 1) + dot(two, o_ref[...], 1, 1)
        mean_ref[...] = mean[:2]
        part_ref[...] = split_dot(mean, w_ref[...], 1, 0)[:2]


def heads_kernel(
    bins_ref,
    flags_ref,
    last_ref,
    sum_ref,
    head_ref,
    w_ref,
    loss_ref,
    logit_ref,
    pooled_grad_ref,
    pooled_ref,
    shift_ref,
    scratch,
):
    scratch[...] = jnp.zeros_like(scratch)
    scratch[0:2, :] = sum_ref[...]
    pooled = scratch[...]
    pooled_ref[...] = pooled[:2]
    width = pooled.shape[1]
    scale = lax.rsqrt(jnp.sum(pooled * pooled, axis=1, keepdims=True) / width + 1e-05)
    logits = scale * split_dot(pooled, head_ref[...], 1, 0)
    rows = lax.broadcasted_iota(jnp.int32, (16, 1), 0)
    col = lax.broadcasted_iota(jnp.int32, logits.shape, 1)
    bins = logits.shape[1] - 1

    def pick(ref):
        return jnp.where(rows == 0, ref[0], ref[1])

    flags = pick(flags_ref)
    live = (rows < 2) & (flags != 2) & ((rows != 1) | (last_ref[0] == 0))
    live = jnp.where(live, 1.0, 0.0)
    target = jnp.where(flags == 1, 1.0, 0.0)
    is_bin = col < bins
    onehot = jnp.where(col == pick(bins_ref), 1.0, 0.0)
    top = jnp.max(jnp.where(is_bin, logits, -1e30), axis=1, keepdims=True)
    e = jnp.where(is_bin, jnp.exp(logits - top), 0.0)
    e_sum = jnp.sum(e, axis=1, keepdims=True)
    reward_loss = live * (jnp.log(e_sum) + top - jnp.sum(onehot * logits, axis=1, keepdims=True))
    term = jnp.sum(jnp.where(is_bin, 0.0, logits), axis=1, keepdims=True)
    small = jnp.exp(-jnp.abs(term))
    term_loss = live * (jnp.maximum(term, 0.0) + jnp.log1p(small) - target * term)
    sigmoid = jnp.where(term >= 0.0, 1.0, small) / (1.0 + small)
    grad = live * jnp.where(is_bin, e / e_sum - onehot, sigmoid - target)
    lane = lax.broadcasted_iota(jnp.int32, (16, 128), 1)
    loss_ref[...] = jnp.where(lane == 0, reward_loss, term_loss)[:8]
    scale_grad = jnp.sum(grad * logits, axis=1, keepdims=True) / scale
    through = scale * split_dot(grad, head_ref[...], 1, 1)
    pooled_grad = through - scale_grad * scale**3 * pooled / width
    logit_ref[...] = (scale * grad)[:2]
    pooled_grad_ref[...] = pooled_grad[:2]
    shift = pooled_grad / PATCHES
    high = shift.astype(BF16)
    low = (shift - high.astype(F32)).astype(BF16)
    shift_ref[...] = dot(w_ref[...], high, 1, 1) + dot(w_ref[...], low, 1, 1)


def backward_kernel(pair, q_ref, ka_ref, kb_ref, va_ref, vb_ref, p_ref, g_ref, shift_ref, *rest):
    if pair:
        dq_ref, da_ref, db_ref = rest
    else:
        add_ref, dq_ref, da_ref, db_ref = rest
    span = PATCHES
    step = 256
    k_cols = jnp.concatenate([ka_ref[...], kb_ref[...]], 1)
    v_rows = jnp.concatenate([va_ref[...], vb_ref[...]], 1).T
    lane = lax.broadcasted_iota(jnp.int32, shift_ref.shape, 1)
    shift = jnp.sum(jnp.where(lane == pair, shift_ref[...], 0.0), axis=1, keepdims=True)
    dk = jnp.zeros((HD, 2 * span), F32)
    dv = jnp.zeros((HD, 2 * span), F32)
    for at in range(0, span, step):
        g = (g_ref[:, at : at + step] + shift).astype(BF16)
        p_low = p_ref[:, at : at + step]
        p = p_low.astype(F32)
        dp = dot(v_rows, g, 1, 0)
        dv = dv + dot(g, p_low, 1, 1)
        delta = jnp.sum(p * dp, axis=0, keepdims=True)
        ds = (p * (dp - delta) * HD ** (-0.5)).astype(BF16)
        dq_ref[at : at + step, :] = dot(k_cols, ds, 1, 0).T.astype(BF16)
        dk = dk + dot(q_ref[:, at : at + step], ds, 1, 1)
    first = jnp.concatenate([dk[:, :span].T, dv[:, :span].T], 1)
    second = jnp.concatenate([dk[:, span:].T, dv[:, span:].T], 1)
    da_ref[...] = first
    if pair:
        db_ref[...] = second.astype(BF16)
    else:
        db_ref[...] = (second + add_ref[...]).astype(BF16)


def out_kernel(og_ref, pooled_grad_ref, t0_ref, t1_ref, mean_ref, out_ref):
    span = PATCHES
    total = dot(og_ref[:, :span], t0_ref[...], 1, 0) + dot(og_ref[:, span:], t1_ref[...], 1, 0)
    for pair in range(2):
        total = total + pooled_grad_ref[:, pair : pair + 1] * mean_ref[pair : pair + 1, :]
    out_ref[...] = total.astype(BF16)


def order_kernel(owners_ref, q_ref, k_ref, v_ref, near_ref, far_ref, scratch):
    n = q_ref.shape[0] // 16
    for piece, out_ref in enumerate((near_ref, far_ref)):
        for i in range(8):
            first = pl.multiple_of(owners_ref[8 * piece + i] * n, n)
            for j, ref in enumerate((q_ref, k_ref, v_ref)):
                scratch[i * n : (i + 1) * n, j * HD : (j + 1) * HD] = ref[pl.ds(first, n), :]
        out_ref[...] = scratch[...].T


def near_kernel(*refs):
    *x_refs, w_ref, all_ref, out_ref = refs
    n = x_refs[0].shape[0]
    for i, ref in enumerate(x_refs):
        all_ref[i * n : (i + 1) * n, :] = ref[...]
    for at in range(0, 2 * PATCHES, PATCHES):
        out_ref[:, at : at + PATCHES] = dot(w_ref[...], all_ref[:, at : at + PATCHES], 1, 0)


def far_kernel(*refs):
    *x_refs, w_ref, near_ref, _, _, _, _, all_ref, kv0_ref, q0_ref, qkv1_ref = refs
    n = x_refs[0].shape[0]
    for i, ref in enumerate(x_refs):
        all_ref[i * n : (i + 1) * n, :] = ref[...]
    span = PATCHES
    first = near_ref[:, :span] + dot(w_ref[...], all_ref[:, :span], 1, 0)
    q0_ref[...] = first[:HD].astype(BF16)
    kv0_ref[...] = first[HD:].astype(BF16)
    second = near_ref[:, span:] + dot(w_ref[...], all_ref[:, span:], 1, 0)
    qkv1_ref[...] = second.astype(BF16)


def call(kernel, out_shape, specs, scratch=(), flops=0, bytes_accessed=0):
    return pl.pallas_call(
        kernel,
        out_shape=[jax.ShapeDtypeStruct(*o) for o in out_shape],
        in_specs=specs,
        out_specs=[VMEM] * len(out_shape),
        scratch_shapes=list(scratch),
        compiler_params=pltpu.CompilerParams(vmem_limit_bytes=24 * 1024 * 1024),
        cost_estimate=pl.CostEstimate(flops=flops, bytes_accessed=bytes_accessed, transcendentals=0),
    )


def local(
    frames,
    w_query,
    w_key,
    w_value,
    w_out,
    head_gain,
    reward_weight,
    term_weight,
    out_grad,
    reward_bins,
    episode_flags,
):
    rows, local_width = frames.shape
    span = PATCHES
    full_width = w_out.shape[1]
    n_tensor = lax.axis_size("tensor")
    position = lax.axis_index("tm")
    me = lax.axis_index("tensor")
    is_last = (position == lax.axis_size("tm") - 1).astype(jnp.int32).reshape(1)
    bins = reward_weight.shape[1]

    def gather(x):
        return lax.all_gather(x, "tensor", axis=0, tiled=True)

    head_local = jnp.concatenate([reward_weight, term_weight[:, None]], 1)
    head_sent = (head_gain[:, None] * head_local).astype(BF16)
    frames_t, head_sent = lax.optimization_barrier((frames.T, head_sent))
    head_full = gather(head_sent)
    frame_mean = frames.astype(F32).reshape(2, span, local_width).mean(axis=1)
    frame_mean = lax.dynamic_update_slice_in_dim(
        jnp.zeros((2, full_width), F32), frame_mean, me * local_width, 1
    )
    owners = [slot_owner(me, s) for s in range(n_tensor)]
    eight = n_tensor // 2 * local_width
    w_pieces = call(
        order_kernel,
        [((3 * HD, eight), BF16)] * 2,
        [SMEM] + [VMEM] * 3,
        [pltpu.VMEM((eight, 3 * HD), BF16)],
        bytes_accessed=5 << 20,
    )(jnp.stack(owners).astype(jnp.int32), w_query, w_key, w_value)
    grad_t = out_grad.T
    w_send = w_out.T.reshape(n_tensor, local_width, HD)

    project_flops = 2 * eight * 3 * HD * rows

    def project_near(near, beside):
        return call(
            near_kernel,
            [((eight, rows), BF16), ((3 * HD, rows), F32)],
            [VMEM] * 9,
            flops=project_flops,
            bytes_accessed=12 << 20,
        )(*near, beside[1][0])

    far, (frame_mean, w_pieces, grad_t, w_send), (x_near, qkv_near) = gather_hierarchical(
        frames_t, (frame_mean, w_pieces, grad_t, w_send), project_near
    )
    corners = tuple(x[:16, :HD] for x in far[:4])
    grad_t, head_full, corners = lax.optimization_barrier((grad_t, head_full, corners))
    og = gather(grad_t)
    x_far, kv0, q0, qkv1 = call(
        far_kernel,
        [
            ((eight, rows), BF16),
            ((2 * HD, span), BF16),
            ((HD, span), BF16),
            ((3 * HD, span), BF16),
        ],
        [VMEM] * 14,
        flops=project_flops,
        bytes_accessed=12 << 20,
    )(*far, w_pieces[1], qkv_near, *corners)
    kv_next = from_behind(kv0, -1)
    q1, kv1 = qkv1[:HD], qkv1[HD:]
    attention_flops = 2 * 2 * span * 2 * span * HD
    o_shape = ((HD, span), BF16)
    t_shape = ((span, HD), BF16)
    p_shape = ((2 * span, span), BF16)
    o0, t0, p0 = call(
        functools.partial(forward_kernel, 0),
        [o_shape, t_shape, p_shape],
        [VMEM] * 5,
        flops=attention_flops,
        bytes_accessed=3 << 20,
    )(q0, kv0[:HD], kv1[:HD], kv0[HD:], kv1[HD:])
    o1, t1, p1, att_mean, part = call(
        functools.partial(forward_kernel, 1),
        [o_shape, t_shape, p_shape, ((2, HD), F32), ((2, full_width), F32)],
        [VMEM] * 5 + [SMEM, VMEM, VMEM],
        flops=attention_flops,
        bytes_accessed=3 << 20,
    )(q1, kv1[:HD], kv_next[:HD], kv1[HD:], kv_next[HD:], is_last, o0, w_out)
    att = jnp.concatenate([o0, o1], 1)
    pooled_sum = sum_over_tensor(part + frame_mean)
    loss, logit_grad, pooled_grad, pooled, shift = call(
        heads_kernel,
        [
            ((8, 128), F32),
            ((2, bins + 1), F32),
            ((2, full_width), F32),
            ((2, full_width), F32),
            ((HD, 16), F32),
        ],
        [SMEM] * 3 + [VMEM] * 3,
        [pltpu.VMEM((16, full_width), F32)],
        flops=1 << 24,
        bytes_accessed=3 << 20,
    )(reward_bins, episode_flags, is_last, pooled_sum, head_full, w_out)
    pair_losses = loss[:2, :2].T

    def mine(a):
        return lax.dynamic_slice_in_dim(a, me * local_width, local_width, 1)

    att_sent, og, shift = lax.optimization_barrier((att, og, shift))
    att_full = gather(att_sent)
    g1 = dot(w_out, og[:, span:], 1, 0)
    g0 = dot(w_out, og[:, :span], 1, 0)

    def backward(pair, q, ka, kb, va, vb, p, g, *add):
        return call(
            functools.partial(backward_kernel, pair),
            [t_shape, ((span, 2 * HD), F32), ((span, 2 * HD), BF16)],
            [VMEM] * (8 + len(add)),
        )(q, ka, kb, va, vb, p, g, shift, *add)

    dq1, d_first1, d_next = backward(
        1, q1, kv1[:HD], kv_next[:HD], kv1[HD:], kv_next[HD:], p1, g1
    )
    returned = from_behind(d_next, 1)
    dq0, d_first0, d1 = backward(
        0, q0, kv0[:HD], kv1[:HD], kv0[HD:], kv1[HD:], p0, g0, d_first1
    )
    w_send, dq0, pooled, logit_grad = lax.optimization_barrier((w_send, dq0, pooled, logit_grad))
    w_cols = lax.all_to_all(w_send, "tensor", split_axis=0, concat_axis=0)
    d0 = (d_first0 + returned.astype(F32)).astype(BF16)
    d_all = jnp.concatenate(
        [jnp.concatenate([dq0, d0], 1), jnp.concatenate([dq1, d1], 1)], 0
    )

    def weight_grads(columns):
        parts = [dot(x, d_all[:, columns], 1, 0).astype(BF16) for x in (x_near, x_far)]
        return jnp.concatenate(parts, 0).reshape(n_tensor, local_width, -1)

    grad_t_qk, grad_t_v = weight_grads(slice(0, 2 * HD)), weight_grads(slice(2 * HD, 3 * HD))
    step_rows = 4 * local_width
    grad_t_out = pl.pallas_call(
        out_kernel,
        grid=(full_width // step_rows,),
        in_specs=[
            pl.BlockSpec((step_rows, rows), lambda i: (i, 0)),
            pl.BlockSpec((step_rows, 2), lambda i: (i, 0)),
            pl.BlockSpec((span, HD), lambda i: (0, 0)),
            pl.BlockSpec((span, HD), lambda i: (0, 0)),
            VMEM,
        ],
        out_specs=pl.BlockSpec((step_rows, HD), lambda i: (i, 0)),
        out_shape=jax.ShapeDtypeStruct((full_width, HD), BF16),
        compiler_params=pltpu.CompilerParams(vmem_limit_bytes=16 * 1024 * 1024),
        cost_estimate=pl.CostEstimate(flops=0, bytes_accessed=0, transcendentals=0),
    )(og, pooled_grad.T, t0, t1, att_mean)
    grad_t_out = grad_t_out.reshape(n_tensor, local_width, HD)

    pooled_mine = mine(pooled)
    gained = pooled_mine * head_gain[None, :]
    gain_in = jnp.dot(logit_grad, head_local.T, precision=lax.Precision.HIGHEST)
    gain_part = jnp.sum(pooled_mine * gain_in, axis=0, keepdims=True)
    small = jnp.concatenate([gained, gain_part], 0)
    small = jnp.pad(small, ((0, 0), (0, bins + 1 - local_width)))
    small = jnp.concatenate([small, logit_grad, jnp.zeros((3, bins + 1), F32)], 0)
    small_high = small.astype(BF16)
    small_low = (small - small_high.astype(F32)).astype(BF16)
    small = jnp.concatenate([small_high, small_low], 0)
    idx = ring_indices(position, me)
    def project_out(cols):
        cols = jnp.transpose(cols, (1, 0, 2)).reshape(local_width, n_tensor * HD)
        return (frames.astype(F32) + dot(att_full, cols, 0, 1)).astype(BF16)

    (qk, _), (vo, packed), mixed = scatter_over_tm(
        Ring(idx, [grad_t_qk], [], None, position),
        Ring(idx, [grad_t_v], [grad_t_out], small, position),
        w_cols,
        project_out,
    )
    packed = packed.astype(F32).reshape(-1, 2, 8, bins + 1)
    packed = packed[:, 0] + packed[:, 1]
    grad_query, grad_key = qk[:, :HD], qk[:, HD:]
    grad_value, grad_out = vo[:, :HD], vo[:, HD:].T
    gained_all = packed[:, :2, :local_width].reshape(-1, local_width)
    logit_all = packed[:, 3:5].reshape(-1, bins + 1)
    head_grad = lax.dot_general(
        gained_all,
        logit_all,
        (((0,), (0,)), ((), ())),
        precision=lax.Precision.HIGHEST,
        preferred_element_type=F32,
    )
    grad_gain = jnp.sum(packed[:, 2, :local_width], axis=0)
    return (
        mixed,
        pair_losses,
        grad_query,
        grad_key,
        grad_value,
        grad_out,
        head_grad[:, :bins],
        head_grad[:, bins],
        grad_gain,
    )


def solution(mesh):
    return jax.shard_map(
        local,
        mesh=mesh,
        in_specs=(
            P("tm", "tensor"),
            P(None, "tensor"),
            P(None, "tensor"),
            P(None, "tensor"),
            P("tensor", None),
            P("tensor"),
            P("tensor", None),
            P("tensor"),
            P("tm", "tensor"),
            P("tm"),
            P("tm"),
        ),
        out_specs=(
            P("tm", "tensor"),
            P(None, "tm"),
            P("tm", "tensor"),
            P("tm", "tensor"),
            P("tm", "tensor"),
            P("tensor", "tm"),
            P("tensor", None),
            P("tensor"),
            P("tensor"),
        ),
        check_vma=False,
    )
```

```python
import functools

import jax
import jax.numpy as jnp
from jax import lax
from jax.experimental import pallas as pl
from jax.experimental.pallas import tpu as pltpu
from jax.sharding import PartitionSpec as P

HD = 128
PATCHES = 512
NY, NX, NC = 4, 2, 2
NH, NZ = 2, 8
F32 = jnp.float32
BF16 = jnp.bfloat16
VMEM = pl.BlockSpec(memory_space=pltpu.VMEM)
SMEM = pl.BlockSpec(memory_space=pltpu.SMEM)
LOG2E = 1.4426950408889634


def dot(a, b, ca, cb):
    return lax.dot_general(a, b, (((ca,), (cb,)), ((), ())), preferred_element_type=F32)


def split_dot(a, b, ca, cb):
    high = a.astype(BF16)
    low = (a - high.astype(F32)).astype(BF16)
    return dot(high, b, ca, cb) + dot(low, b, ca, cb)


def tensor_permute(x, move):
    pairs = []
    for y in range(NY):
        for h in range(NX):
            for c in range(NC):
                y2, h2, c2 = move(y, h, c)
                pairs.append(((y * NX + h) * NC + c, (y2 * NX + h2) * NC + c2))
    return lax.ppermute(x, "tensor", pairs)


def tm_permute(x, move):
    pairs = []
    for h in range(NH):
        for z in range(NZ):
            h2, z2 = move(h, z)
            pairs.append((h * NZ + z, h2 * NZ + z2))
    return lax.ppermute(x, "tm", pairs)


def from_behind(x, by):
    size = NH * NZ
    return lax.ppermute(x, "tm", [(i, i + by) for i in range(size) if 0 <= i + by < size])


def sum_over_tensor(x):
    x = x + tensor_permute(x, lambda y, h, c: (y, h, c ^ 1))
    across = tensor_permute(x, lambda y, h, c: (y, h ^ 1, c))
    beside = tensor_permute(x, lambda y, h, c: (y ^ 1, h, c))
    both = tensor_permute(x, lambda y, h, c: (y ^ 1, h ^ 1, c))
    x = (x + across) + (beside + both)
    return x, tensor_permute(x, lambda y, h, c: (3 - y, h, c))


ORDER = ((0, 0), (0, 1), (1, 0), (3, 0), (3, 1), (1, 1), (2, 0), (2, 1))


def slot_owner(me, slot):
    (y, x), core = ORDER[slot // 8 * 4 + slot % 4], slot // 4 % 2
    my_y, my_x, my_core = me // (NX * NC), me // NC % NX, me % NC
    return (lax.rem(my_y + y, NY) * NX + (my_x ^ x)) * NC + (my_core ^ core)


def owner_slot(me, owner):
    y = lax.rem(owner // (NX * NC) + NY - me // (NX * NC), NY)
    x = (owner // NC % NX) ^ (me // NC % NX)
    place = 0
    for i, (its_y, its_x) in enumerate(ORDER):
        place = place + jnp.where((y == its_y) & (x == its_x), i // 4 * 8 + i % 4, 0)
    return place + 4 * ((owner % NC) ^ (me % NC))


def gather_hierarchical(part, beside, use_near):
    def up(x):
        return tensor_permute(x, lambda y, h, c: ((y + 1) % NY, h, c))

    def down(x):
        return tensor_permute(x, lambda y, h, c: ((y - 1) % NY, h, c))

    def across(x):
        return tensor_permute(x, lambda y, h, c: (y, h ^ 1, c))

    def swap(x):
        return tensor_permute(x, lambda y, h, c: (y, h, c ^ 1))

    below, above, pair, part_other = up(part), down(part), across(part), swap(part)
    below, above, pair, part_other, beside = lax.optimization_barrier(
        (below, above, pair, part_other, beside)
    )
    pair_below, pair_above, opposite = up(pair), down(pair), up(below)
    near = (part, pair, above, below, part_other, swap(pair), swap(above), swap(below))
    pair_above, used = lax.optimization_barrier((pair_above, use_near(near, beside)))
    far = (pair_below, pair_above, opposite, down(pair_above))
    return far + tuple(swap(x) for x in far), beside, used


def add_parts(out_ref, row, parts, received=()):
    n = parts[0].shape[1]
    at = 0
    for part in parts:
        columns = slice(at, at + part.shape[2])
        at += part.shape[2]
        total = part[0]
        if received:
            total = total.astype(F32)
            for ref, first in received:
                total = total + ref[first : first + n, columns].astype(F32)
        out_ref[row : row + n, columns] = total.astype(out_ref.dtype)


def ring_first_kernel(count, idx_ref, *refs):
    parts, (*extra, r_ref, l_ref) = refs[: 2 * count], refs[2 * count :]
    n = parts[0].shape[1]
    for h, out_ref in enumerate((r_ref, l_ref)):
        add_parts(out_ref, 0, parts[h * count : (h + 1) * count])
        for ref in extra:
            out_ref[n:, :] = ref[...]


def ring_step_kernel(count, first, idx_ref, r_in, l_in, *refs):
    parts, outs = refs[: 4 * count], refs[4 * count :]
    n = parts[0].shape[1]
    for side, (received, out_ref) in enumerate(zip((r_in, l_in), outs)):
        for h in range(NH):
            block = parts[(2 * side + h) * count : (2 * side + h + 1) * count]
            if first:
                add_parts(out_ref, h * n, block, [(received, 0)] if h == side else [])
            else:
                add_parts(out_ref, h * n, block, [(received, h * n)])
        few = out_ref.shape[0] - 2 * n
        if few:
            extra = received[received.shape[0] - few :, :]
            out_ref[2 * n :, :] = extra
            outs[2 + side][...] = extra


def ring_last_kernel(count, idx_ref, r_in, l_in, *refs):
    parts, (*extras, mine_ref, theirs_ref, scratch) = refs[: 2 * count], refs[2 * count :]
    n = parts[0].shape[1]
    few = extras[0].shape[0] if extras else 0
    extras = [ref[...] for ref in extras]
    if few:
        extras.insert(NZ // 2, r_in[2 * n :, :])
    for h in range(NH):
        block = parts[h * count : (h + 1) * count]
        add_parts(scratch, h * n, block, [(r_in, h * n), (l_in, h * n)])
    upper = idx_ref[0] == 1
    low, high = scratch[:n, :], scratch[n:, :]
    mine_ref[...] = jnp.where(upper, high, low)
    theirs_ref[:n, :] = jnp.where(upper, low, high).astype(BF16)
    z = idx_ref[1]
    shifts = [0] + [-1 - k for k in range(NZ // 2)] + [1 + k for k in range(NZ // 2 - 1)]
    for shift, extra in zip(shifts, extras):
        owner = lax.rem(z + NZ + shift, NZ)
        theirs_ref[pl.ds(pl.multiple_of(n + few * owner, few), few), :] = extra


def ring_indices(position, me):
    z = lax.rem(position, NZ)
    half = NZ // 2
    idx = [(position >= NZ).astype(jnp.int32), z]
    for distance in range(half, -1, -1):
        owners = [
            h * NZ + lax.rem(z + NZ + sign * distance, NZ) for sign in (1, -1) for h in range(NH)
        ]
        idx += [owner_slot(me, owner) for owner in owners] + owners
    return jnp.stack([i.astype(jnp.int32) for i in idx])


class Ring:
    def __init__(self, idx, by_slot, by_owner, extra, position):
        self.idx, self.position = idx, position
        self.arrays = [(x, 0) for x in by_slot] + [(x, 4) for x in by_owner]
        self.n = self.arrays[0][0].shape[1]
        self.columns = sum(x.shape[2] for x, _ in self.arrays)
        self.extras = [] if extra is None else [extra]
        self.few = sum(x.shape[0] for x in self.extras)
        self.rights, self.lefts = [], []

    def blocks(self, step, number):
        def place(which):
            return lambda i, idx: (idx[2 + 8 * step + which], 0, 0)

        specs, args = [], []
        for k in range(number):
            for x, base in self.arrays:
                specs.append(pl.BlockSpec((1,) + x.shape[1:], place(base + k)))
                args.append(x)
        return specs, args

    def run(self, kernel, after, specs, args, out_shape, scratch=()):
        def body(idx_ref, _, *refs):
            kernel(len(self.arrays), idx_ref, *refs)

        return pl.pallas_call(
            body,
            grid_spec=pltpu.PrefetchScalarGridSpec(
                num_scalar_prefetch=1,
                grid=(1,),
                in_specs=[pl.BlockSpec(memory_space=pl.ANY)] + specs,
                out_specs=[VMEM] * len(out_shape),
                scratch_shapes=list(scratch),
            ),
            out_shape=[jax.ShapeDtypeStruct(*o) for o in out_shape],
            compiler_params=pltpu.CompilerParams(vmem_limit_bytes=16 * 1024 * 1024),
            cost_estimate=pl.CostEstimate(flops=5 << 30, bytes_accessed=2 << 20, transcendentals=0),
        )(self.idx, after, *args)

    def send(self):
        self.r = tm_permute(self.r, lambda h, z: (h, (z + 1) % NZ))
        self.l = tm_permute(self.l, lambda h, z: (h, (z - 1) % NZ))

    def first(self, after):
        specs, args = self.blocks(0, 2)
        self.r, self.l = self.run(
            ring_first_kernel,
            after,
            specs + [VMEM] * len(self.extras),
            args + self.extras,
            [((self.n + self.few, self.columns), BF16)] * 2,
        )

    def step(self, step, after):
        specs, args = self.blocks(step, 4)

        def kernel(count, *refs):
            ring_step_kernel(count, step == 1, *refs)

        few = [((self.few, self.columns), BF16)] * 2 if self.few else []
        self.r, self.l, *passed = self.run(
            kernel,
            after,
            [VMEM] * 2 + specs,
            [self.r, self.l] + args,
            [((2 * self.n + self.few, self.columns), BF16)] * 2 + few,
        )
        self.rights += passed[:1]
        self.lefts += passed[1:]

    def last(self, after):
        few, columns = self.few, self.columns
        specs, args = self.blocks(NZ // 2, 2)
        passed = self.rights + self.lefts
        self.mine, self.r = self.run(
            ring_last_kernel,
            after,
            [VMEM] * 2 + specs + [VMEM] * len(self.extras + passed),
            [self.r, self.l] + args + self.extras + passed,
            [((self.n, columns), F32), ((self.n + NZ * few, columns), BF16)],
            [pltpu.VMEM((2 * self.n, columns), F32)],
        )

    def exchange(self):
        return tm_permute(self.r, lambda h, z: (h ^ 1, z))

    def finish(self, other):
        upper = self.position >= NZ
        total = self.mine + other[: self.n].astype(F32)
        if not self.few:
            return total, None
        theirs, other = self.r[self.n :], other[self.n :]
        gathered = [jnp.where(upper, other, theirs), jnp.where(upper, theirs, other)]
        return total, jnp.concatenate(gathered, 0)


def scatter_over_tm(one, two, beside, late):
    half = NZ // 2
    one.first(one.idx)
    two.first(one.r)
    for step in range(1, half + 1):
        before = two.r
        one.send()
        two.send()
        if step < half:
            one.step(step, before)
            two.step(step, one.r)
        else:
            one.last(before)
            two.last(one.r)
    others = one.exchange(), two.exchange()
    others, result = lax.optimization_barrier((others, late(beside)))
    return one.finish(others[0]), two.finish(others[1]), result


def forward_kernel(pair, q_ref, ka_ref, kb_ref, va_ref, vb_ref, *rest):
    if pair:
        last_ref, first_ref, w_ref, own_ref, o_ref, t_ref, p_ref, mean_ref, part_ref = rest
    else:
        o_ref, t_ref, p_ref = rest
    span = PATCHES
    step = 256
    k_rows = jnp.concatenate([ka_ref[...], kb_ref[...]], 1).T
    v_cols = jnp.concatenate([va_ref[...], vb_ref[...]], 1)
    for at in range(0, span, step):
        s = dot(k_rows, q_ref[:, at : at + step], 1, 0) * (HD ** (-0.5) * LOG2E)
        if pair:
            key = lax.broadcasted_iota(jnp.int32, s.shape, 0)
            s = jnp.where((key >= span) & (last_ref[0] == 1), -1e30, s)
        e = jnp.exp2(s - jnp.max(s, axis=0, keepdims=True))
        p = (e * (1.0 / jnp.sum(e, axis=0, keepdims=True))).astype(BF16)
        p_ref[:, at : at + step] = p
        o = dot(v_cols, p, 1, 0)
        o_ref[:, at : at + step] = o.astype(BF16)
        t_ref[at : at + step, :] = o.T.astype(BF16)
    if pair:
        row = lax.broadcasted_iota(jnp.int32, (16, span), 0)
        one = (jnp.where(row == 0, 1.0, 0.0) / span).astype(BF16)
        two = (jnp.where(row == 1, 1.0, 0.0) / span).astype(BF16)
        mean = dot(one, first_ref[...], 1, 1) + dot(two, o_ref[...], 1, 1)
        mean_ref[...] = mean[:2]
        part = split_dot(mean, w_ref[...], 1, 0)[:2] + own_ref[...]
        width = part_ref.shape[1]
        for i in range(4):
            part_ref[2 * i : 2 * i + 2, :] = part[:, i * width : (i + 1) * width]


def heads_kernel(
    bins_ref,
    flags_ref,
    last_ref,
    one_ref,
    two_ref,
    head_ref,
    w_ref,
    loss_ref,
    logit_ref,
    pooled_grad_ref,
    pooled_ref,
    shift_ref,
    scratch,
):
    scratch[...] = jnp.zeros_like(scratch)
    total = one_ref[...] + two_ref[...]
    part_width = total.shape[1]
    for i in range(4):
        scratch[0:2, i * part_width : (i + 1) * part_width] = total[2 * i : 2 * i + 2]
    pooled = scratch[...]
    pooled_ref[...] = pooled[:2]
    width = pooled.shape[1]
    scale = lax.rsqrt(jnp.sum(pooled * pooled, axis=1, keepdims=True) / width + 1e-05)
    logits = scale * split_dot(pooled, head_ref[...], 1, 0)
    rows = lax.broadcasted_iota(jnp.int32, (16, 1), 0)
    col = lax.broadcasted_iota(jnp.int32, logits.shape, 1)
    bins = logits.shape[1] - 1

    def pick(ref):
        return jnp.where(rows == 0, ref[0], ref[1])

    flags = pick(flags_ref)
    live = (rows < 2) & (flags != 2) & ((rows != 1) | (last_ref[0] == 0))
    live = jnp.where(live, 1.0, 0.0)
    target = jnp.where(flags == 1, 1.0, 0.0)
    is_bin = col < bins
    onehot = jnp.where(col == pick(bins_ref), 1.0, 0.0)
    top = jnp.max(jnp.where(is_bin, logits, -1e30), axis=1, keepdims=True)
    e = jnp.where(is_bin, jnp.exp(logits - top), 0.0)
    e_sum = jnp.sum(e, axis=1, keepdims=True)
    reward_loss = live * (jnp.log(e_sum) + top - jnp.sum(onehot * logits, axis=1, keepdims=True))
    term = jnp.sum(jnp.where(is_bin, 0.0, logits), axis=1, keepdims=True)
    small = jnp.exp(-jnp.abs(term))
    term_loss = live * (jnp.maximum(term, 0.0) + jnp.log1p(small) - target * term)
    sigmoid = jnp.where(term >= 0.0, 1.0, small) / (1.0 + small)
    grad = live * jnp.where(is_bin, e / e_sum - onehot, sigmoid - target)
    lane = lax.broadcasted_iota(jnp.int32, (16, 128), 1)
    loss_ref[...] = jnp.where(lane == 0, reward_loss, term_loss)[:8]
    scale_grad = jnp.sum(grad * logits, axis=1, keepdims=True) / scale
    through = scale * split_dot(grad, head_ref[...], 1, 1)
    pooled_grad = through - scale_grad * scale**3 * pooled / width
    logit_ref[...] = (scale * grad)[:2]
    pooled_grad_ref[...] = pooled_grad[:2]
    shift = pooled_grad / PATCHES
    high = shift.astype(BF16)
    low = (shift - high.astype(F32)).astype(BF16)
    shift_ref[...] = dot(w_ref[...], high, 1, 1) + dot(w_ref[...], low, 1, 1)


def backward_kernel(pair, q_ref, ka_ref, kb_ref, va_ref, vb_ref, p_ref, g_ref, shift_ref, *rest):
    if pair:
        dq_ref, da_ref, db_ref = rest
    else:
        add_ref, dq_ref, da_ref, db_ref = rest
    span = PATCHES
    step = 256
    k_cols = jnp.concatenate([ka_ref[...], kb_ref[...]], 1)
    v_rows = jnp.concatenate([va_ref[...], vb_ref[...]], 1).T
    lane = lax.broadcasted_iota(jnp.int32, shift_ref.shape, 1)
    shift = jnp.sum(jnp.where(lane == pair, shift_ref[...], 0.0), axis=1, keepdims=True)
    dk = jnp.zeros((HD, 2 * span), F32)
    dv = jnp.zeros((HD, 2 * span), F32)
    for at in range(0, span, step):
        first = pair * span + at
        g = (g_ref[:, first : first + step] + shift).astype(BF16)
        p_low = p_ref[:, at : at + step]
        p = p_low.astype(F32)
        dp = dot(v_rows, g, 1, 0)
        dv = dv + dot(g, p_low, 1, 1)
        delta = jnp.sum(p * dp, axis=0, keepdims=True)
        ds = (p * (dp - delta) * HD ** (-0.5)).astype(BF16)
        dq_ref[at : at + step, :] = dot(k_cols, ds, 1, 0).T.astype(BF16)
        dk = dk + dot(q_ref[:, at : at + step], ds, 1, 1)
    first = jnp.concatenate([dk[:, :span].T, dv[:, :span].T], 1)
    second = jnp.concatenate([dk[:, span:].T, dv[:, span:].T], 1)
    da_ref[...] = first
    if pair:
        db_ref[...] = second.astype(BF16)
    else:
        db_ref[...] = (second + add_ref[...]).astype(BF16)


def og_kernel(og_ref, w_ref, pooled_grad_ref, t0_ref, t1_ref, mean_ref, g_ref, out_ref):
    span = PATCHES

    @pl.when(pl.program_id(0) == 0)
    def _():
        g_ref[...] = jnp.zeros_like(g_ref)

    total = dot(og_ref[:, :span], t0_ref[...], 1, 0) + dot(og_ref[:, span:], t1_ref[...], 1, 0)
    for pair in range(2):
        total = total + pooled_grad_ref[:, pair : pair + 1] * mean_ref[pair : pair + 1, :]
    out_ref[...] = total.astype(BF16)
    g_ref[...] += dot(w_ref[...], og_ref[...], 1, 0)


def order_kernel(owners_ref, q_ref, k_ref, v_ref, near_ref, far_ref, scratch):
    n = q_ref.shape[0] // 16
    for piece, out_ref in enumerate((near_ref, far_ref)):
        for i in range(8):
            first = pl.multiple_of(owners_ref[8 * piece + i] * n, n)
            for j, ref in enumerate((q_ref, k_ref, v_ref)):
                scratch[i * n : (i + 1) * n, j * HD : (j + 1) * HD] = ref[pl.ds(first, n), :]
        out_ref[...] = scratch[...].T


def near_kernel(*refs):
    *x_refs, w_ref, all_ref, out_ref = refs
    n = x_refs[0].shape[0]
    for i, ref in enumerate(x_refs):
        all_ref[i * n : (i + 1) * n, :] = ref[...]
    for at in range(0, 2 * PATCHES, PATCHES):
        out_ref[:, at : at + PATCHES] = dot(w_ref[...], all_ref[:, at : at + PATCHES], 1, 0)


def far_kernel(*refs):
    *x_refs, w_ref, near_ref, _, _, _, _, all_ref, kv0_ref, q0_ref, qkv1_ref = refs
    n = x_refs[0].shape[0]
    for i, ref in enumerate(x_refs):
        all_ref[i * n : (i + 1) * n, :] = ref[...]
    span = PATCHES
    first = near_ref[:, :span] + dot(w_ref[...], all_ref[:, :span], 1, 0)
    q0_ref[...] = first[:HD].astype(BF16)
    kv0_ref[...] = first[HD:].astype(BF16)
    second = near_ref[:, span:] + dot(w_ref[...], all_ref[:, span:], 1, 0)
    qkv1_ref[...] = second.astype(BF16)


def call(kernel, out_shape, specs, scratch=(), flops=0, bytes_accessed=0):
    return pl.pallas_call(
        kernel,
        out_shape=[jax.ShapeDtypeStruct(*o) for o in out_shape],
        in_specs=specs,
        out_specs=[VMEM] * len(out_shape),
        scratch_shapes=list(scratch),
        compiler_params=pltpu.CompilerParams(vmem_limit_bytes=24 * 1024 * 1024),
        cost_estimate=pl.CostEstimate(flops=flops, bytes_accessed=bytes_accessed, transcendentals=0),
    )


def local(
    frames,
    w_query,
    w_key,
    w_value,
    w_out,
    head_gain,
    reward_weight,
    term_weight,
    out_grad,
    reward_bins,
    episode_flags,
):
    rows, local_width = frames.shape
    span = PATCHES
    full_width = w_out.shape[1]
    n_tensor = lax.axis_size("tensor")
    position = lax.axis_index("tm")
    me = lax.axis_index("tensor")
    is_last = (position == lax.axis_size("tm") - 1).astype(jnp.int32).reshape(1)
    bins = reward_weight.shape[1]

    def gather(x):
        return lax.all_gather(x, "tensor", axis=0, tiled=True)

    head_local = jnp.concatenate([reward_weight, term_weight[:, None]], 1)
    head_sent = (head_gain[:, None] * head_local).astype(BF16)
    frames_t, head_sent = lax.optimization_barrier((frames.T, head_sent))
    head_full = gather(head_sent)
    frame_mean = frames.astype(F32).reshape(2, span, local_width).mean(axis=1)
    frame_mean = lax.dynamic_update_slice_in_dim(
        jnp.zeros((2, full_width), F32), frame_mean, me * local_width, 1
    )
    owners = [slot_owner(me, s) for s in range(n_tensor)]
    eight = n_tensor // 2 * local_width
    w_pieces = call(
        order_kernel,
        [((3 * HD, eight), BF16)] * 2,
        [SMEM] + [VMEM] * 3,
        [pltpu.VMEM((eight, 3 * HD), BF16)],
        bytes_accessed=5 << 20,
    )(jnp.stack(owners).astype(jnp.int32), w_query, w_key, w_value)
    grad_t = out_grad.T
    w_send = w_out.T.reshape(n_tensor, local_width, HD)

    project_flops = 2 * eight * 3 * HD * rows

    def project_near(near, beside):
        return call(
            near_kernel,
            [((eight, rows), BF16), ((3 * HD, rows), F32)],
            [VMEM] * 9,
            flops=project_flops,
            bytes_accessed=12 << 20,
        )(*near, beside[1][0])

    far, (frame_mean, w_pieces, grad_t, w_send), (x_near, qkv_near) = gather_hierarchical(
        frames_t, (frame_mean, w_pieces, grad_t, w_send), project_near
    )
    corners = tuple(x[:16, :HD] for x in far[:4])
    grad_t, head_full, corners = lax.optimization_barrier((grad_t, head_full, corners))
    og = gather(grad_t)
    x_far, kv0, q0, qkv1 = call(
        far_kernel,
        [
            ((eight, rows), BF16),
            ((2 * HD, span), BF16),
            ((HD, span), BF16),
            ((3 * HD, span), BF16),
        ],
        [VMEM] * 14,
        flops=project_flops,
        bytes_accessed=12 << 20,
    )(*far, w_pieces[1], qkv_near, *corners)
    kv_next = from_behind(kv0, -1)
    q1, kv1 = qkv1[:HD], qkv1[HD:]
    attention_flops = 2 * 2 * span * 2 * span * HD
    o_shape = ((HD, span), BF16)
    t_shape = ((span, HD), BF16)
    p_shape = ((2 * span, span), BF16)
    o0, t0, p0 = call(
        functools.partial(forward_kernel, 0),
        [o_shape, t_shape, p_shape],
        [VMEM] * 5,
        flops=attention_flops,
        bytes_accessed=3 << 20,
    )(q0, kv0[:HD], kv1[:HD], kv0[HD:], kv1[HD:])
    o1, t1, p1, att_mean, part = call(
        functools.partial(forward_kernel, 1),
        [o_shape, t_shape, p_shape, ((2, HD), F32), ((8, full_width // 4), F32)],
        [VMEM] * 5 + [SMEM, VMEM, VMEM, VMEM],
        flops=attention_flops,
        bytes_accessed=3 << 20,
    )(q1, kv1[:HD], kv_next[:HD], kv1[HD:], kv_next[HD:], is_last, o0, w_out, frame_mean)
    att = jnp.concatenate([o0, o1], 1)
    pooled_sum = sum_over_tensor(part)
    loss, logit_grad, pooled_grad, pooled, shift = call(
        heads_kernel,
        [
            ((8, 128), F32),
            ((2, bins + 1), F32),
            ((2, full_width), F32),
            ((2, full_width), F32),
            ((HD, 16), F32),
        ],
        [SMEM] * 3 + [VMEM] * 4,
        [pltpu.VMEM((16, full_width), F32)],
        flops=1 << 24,
        bytes_accessed=3 << 20,
    )(reward_bins, episode_flags, is_last, *pooled_sum, head_full, w_out)
    pair_losses = loss[:2, :2].T

    def mine(a):
        return lax.dynamic_slice_in_dim(a, me * local_width, local_width, 1)

    att_sent, og, shift = lax.optimization_barrier((att, og, shift))
    att_full = gather(att_sent)
    step_rows = 4 * local_width
    g, grad_t_out = pl.pallas_call(
        og_kernel,
        grid=(full_width // step_rows,),
        in_specs=[
            pl.BlockSpec((step_rows, rows), lambda i: (i, 0)),
            pl.BlockSpec((HD, step_rows), lambda i: (0, i)),
            pl.BlockSpec((step_rows, 2), lambda i: (i, 0)),
            pl.BlockSpec((span, HD), lambda i: (0, 0)),
            pl.BlockSpec((span, HD), lambda i: (0, 0)),
            pl.BlockSpec((2, HD), lambda i: (0, 0)),
        ],
        out_specs=[
            pl.BlockSpec((HD, rows), lambda i: (0, 0)),
            pl.BlockSpec((step_rows, HD), lambda i: (i, 0)),
        ],
        out_shape=[
            jax.ShapeDtypeStruct((HD, rows), F32),
            jax.ShapeDtypeStruct((full_width, HD), BF16),
        ],
        compiler_params=pltpu.CompilerParams(vmem_limit_bytes=48 * 1024 * 1024),
        cost_estimate=pl.CostEstimate(flops=4 << 30, bytes_accessed=8 << 20, transcendentals=0),
    )(og, w_out, pooled_grad.T, t0, t1, att_mean)

    def backward(pair, q, ka, kb, va, vb, p, g, *add):
        return call(
            functools.partial(backward_kernel, pair),
            [t_shape, ((span, 2 * HD), F32), ((span, 2 * HD), BF16)],
            [VMEM] * (8 + len(add)),
        )(q, ka, kb, va, vb, p, g, shift, *add)

    dq1, d_first1, d_next = backward(
        1, q1, kv1[:HD], kv_next[:HD], kv1[HD:], kv_next[HD:], p1, g
    )
    returned = from_behind(d_next, 1)
    dq0, d_first0, d1 = backward(
        0, q0, kv0[:HD], kv1[:HD], kv0[HD:], kv1[HD:], p0, g, d_first1
    )
    w_send, dq0, pooled, logit_grad = lax.optimization_barrier((w_send, dq0, pooled, logit_grad))
    w_cols = lax.all_to_all(w_send, "tensor", split_axis=0, concat_axis=0)
    d0 = (d_first0 + returned.astype(F32)).astype(BF16)
    d_all = jnp.concatenate(
        [jnp.concatenate([dq0, d0], 1), jnp.concatenate([dq1, d1], 1)], 0
    )

    def weight_grads(columns):
        parts = [dot(x, d_all[:, columns], 1, 0).astype(BF16) for x in (x_near, x_far)]
        return jnp.concatenate(parts, 0).reshape(n_tensor, local_width, -1)

    grad_t_qk, grad_t_v = weight_grads(slice(0, 2 * HD)), weight_grads(slice(2 * HD, 3 * HD))
    grad_t_out = grad_t_out.reshape(n_tensor, local_width, HD)

    pooled_mine = mine(pooled)
    gained = pooled_mine * head_gain[None, :]
    gain_in = jnp.dot(logit_grad, head_local.T, precision=lax.Precision.HIGHEST)
    gain_part = jnp.sum(pooled_mine * gain_in, axis=0, keepdims=True)
    small = jnp.concatenate([gained, gain_part], 0)
    small = jnp.pad(small, ((0, 0), (0, bins + 1 - local_width)))
    small = jnp.concatenate([small, logit_grad, jnp.zeros((3, bins + 1), F32)], 0)
    small_high = small.astype(BF16)
    small_low = (small - small_high.astype(F32)).astype(BF16)
    small = jnp.concatenate([small_high, small_low], 0)
    idx = ring_indices(position, me)
    def project_out(cols):
        cols = jnp.transpose(cols, (1, 0, 2)).reshape(local_width, n_tensor * HD)
        return (frames.astype(F32) + dot(att_full, cols, 0, 1)).astype(BF16)

    (qk, _), (vo, packed), mixed = scatter_over_tm(
        Ring(idx, [grad_t_qk], [], None, position),
        Ring(idx, [grad_t_v], [grad_t_out], small, position),
        w_cols,
        project_out,
    )
    packed = packed.astype(F32).reshape(-1, 2, 8, bins + 1)
    packed = packed[:, 0] + packed[:, 1]
    grad_query, grad_key = qk[:, :HD], qk[:, HD:]
    grad_value, grad_out = vo[:, :HD], vo[:, HD:].T
    gained_all = packed[:, :2, :local_width].reshape(-1, local_width)
    logit_all = packed[:, 3:5].reshape(-1, bins + 1)
    head_grad = lax.dot_general(
        gained_all,
        logit_all,
        (((0,), (0,)), ((), ())),
        precision=lax.Precision.HIGHEST,
        preferred_element_type=F32,
    )
    grad_gain = jnp.sum(packed[:, 2, :local_width], axis=0)
    return (
        mixed,
        pair_losses,
        grad_query,
        grad_key,
        grad_value,
        grad_out,
        head_grad[:, :bins],
        head_grad[:, bins],
        grad_gain,
    )


def solution(mesh):
    return jax.shard_map(
        local,
        mesh=mesh,
        in_specs=(
            P("tm", "tensor"),
            P(None, "tensor"),
            P(None, "tensor"),
            P(None, "tensor"),
            P("tensor", None),
            P("tensor"),
            P("tensor", None),
            P("tensor"),
            P("tm", "tensor"),
            P("tm"),
            P("tm"),
        ),
        out_specs=(
            P("tm", "tensor"),
            P(None, "tm"),
            P("tm", "tensor"),
            P("tm", "tensor"),
            P("tm", "tensor"),
            P("tensor", "tm"),
            P("tensor", None),
            P("tensor"),
            P("tensor"),
        ),
        check_vma=False,
    )
```

```python
import functools

import jax
import jax.numpy as jnp
from jax import lax
from jax.experimental import pallas as pl
from jax.experimental.pallas import tpu as pltpu
from jax.sharding import PartitionSpec as P

HD = 128
PATCHES = 512
NY, NX, NC = 4, 2, 2
NH, NZ = 2, 8
F32 = jnp.float32
BF16 = jnp.bfloat16
VMEM = pl.BlockSpec(memory_space=pltpu.VMEM)
SMEM = pl.BlockSpec(memory_space=pltpu.SMEM)
LOG2E = 1.4426950408889634


def dot(a, b, ca, cb):
    return lax.dot_general(a, b, (((ca,), (cb,)), ((), ())), preferred_element_type=F32)


def split_dot(a, b, ca, cb):
    high = a.astype(BF16)
    low = (a - high.astype(F32)).astype(BF16)
    return dot(high, b, ca, cb) + dot(low, b, ca, cb)


def tensor_permute(x, move):
    pairs = []
    for y in range(NY):
        for h in range(NX):
            for c in range(NC):
                y2, h2, c2 = move(y, h, c)
                pairs.append(((y * NX + h) * NC + c, (y2 * NX + h2) * NC + c2))
    return lax.ppermute(x, "tensor", pairs)


def tm_permute(x, move):
    pairs = []
    for h in range(NH):
        for z in range(NZ):
            h2, z2 = move(h, z)
            pairs.append((h * NZ + z, h2 * NZ + z2))
    return lax.ppermute(x, "tm", pairs)


def from_behind(x, by):
    size = NH * NZ
    return lax.ppermute(x, "tm", [(i, i + by) for i in range(size) if 0 <= i + by < size])


def sum_over_tensor(x):
    x = x + tensor_permute(x, lambda y, h, c: (y, h, c ^ 1))
    across = tensor_permute(x, lambda y, h, c: (y, h ^ 1, c))
    beside = tensor_permute(x, lambda y, h, c: (y ^ 1, h, c))
    both = tensor_permute(x, lambda y, h, c: (y ^ 1, h ^ 1, c))
    x = (x + across) + (beside + both)
    return x, tensor_permute(x, lambda y, h, c: (3 - y, h, c))


ORDER = ((0, 0), (0, 1), (1, 0), (3, 0), (3, 1), (1, 1), (2, 0), (2, 1))


def slot_owner(me, slot):
    (y, x), core = ORDER[slot // 8 * 4 + slot % 4], slot // 4 % 2
    my_y, my_x, my_core = me // (NX * NC), me // NC % NX, me % NC
    return (lax.rem(my_y + y, NY) * NX + (my_x ^ x)) * NC + (my_core ^ core)


def owner_slot(me, owner):
    y = lax.rem(owner // (NX * NC) + NY - me // (NX * NC), NY)
    x = (owner // NC % NX) ^ (me // NC % NX)
    place = 0
    for i, (its_y, its_x) in enumerate(ORDER):
        place = place + jnp.where((y == its_y) & (x == its_x), i // 4 * 8 + i % 4, 0)
    return place + 4 * ((owner % NC) ^ (me % NC))


def gather_hierarchical(part, beside, use_near):
    def up(x):
        return tensor_permute(x, lambda y, h, c: ((y + 1) % NY, h, c))

    def down(x):
        return tensor_permute(x, lambda y, h, c: ((y - 1) % NY, h, c))

    def across(x):
        return tensor_permute(x, lambda y, h, c: (y, h ^ 1, c))

    def swap(x):
        return tensor_permute(x, lambda y, h, c: (y, h, c ^ 1))

    below, above, pair, part_other = up(part), down(part), across(part), swap(part)
    below, above, pair, part_other, beside = lax.optimization_barrier(
        (below, above, pair, part_other, beside)
    )
    pair_below, pair_above, opposite = up(pair), down(pair), up(below)
    near = (part, pair, above, below, part_other, swap(pair), swap(above), swap(below))
    pair_above, used = lax.optimization_barrier((pair_above, use_near(near, beside)))
    far = (pair_below, pair_above, opposite, down(pair_above))
    return far + tuple(swap(x) for x in far), beside, used


def add_parts(out_ref, row, parts, received=()):
    n = parts[0].shape[1]
    at = 0
    for part in parts:
        columns = slice(at, at + part.shape[2])
        at += part.shape[2]
        total = part[0]
        if received:
            total = total.astype(F32)
            for ref, first in received:
                total = total + ref[first : first + n, columns].astype(F32)
        out_ref[row : row + n, columns] = total.astype(out_ref.dtype)


def ring_first_kernel(count, idx_ref, *refs):
    parts, (*extra, r_ref, l_ref) = refs[: 2 * count], refs[2 * count :]
    n = parts[0].shape[1]
    for h, out_ref in enumerate((r_ref, l_ref)):
        add_parts(out_ref, 0, parts[h * count : (h + 1) * count])
        for ref in extra:
            out_ref[n:, :] = ref[...]


def ring_step_kernel(count, first, idx_ref, r_in, l_in, *refs):
    parts, outs = refs[: 4 * count], refs[4 * count :]
    n = parts[0].shape[1]
    for side, (received, out_ref) in enumerate(zip((r_in, l_in), outs)):
        for h in range(NH):
            block = parts[(2 * side + h) * count : (2 * side + h + 1) * count]
            if first:
                add_parts(out_ref, h * n, block, [(received, 0)] if h == side else [])
            else:
                add_parts(out_ref, h * n, block, [(received, h * n)])
        few = out_ref.shape[0] - 2 * n
        if few:
            extra = received[received.shape[0] - few :, :]
            out_ref[2 * n :, :] = extra
            outs[2 + side][...] = extra


def ring_last_kernel(count, idx_ref, r_in, l_in, *refs):
    parts, (*extras, mine_ref, theirs_ref, scratch) = refs[: 2 * count], refs[2 * count :]
    n = parts[0].shape[1]
    few = extras[0].shape[0] if extras else 0
    extras = [ref[...] for ref in extras]
    if few:
        extras.insert(NZ // 2, r_in[2 * n :, :])
    for h in range(NH):
        block = parts[h * count : (h + 1) * count]
        add_parts(scratch, h * n, block, [(r_in, h * n), (l_in, h * n)])
    upper = idx_ref[0] == 1
    low, high = scratch[:n, :], scratch[n:, :]
    mine_ref[...] = jnp.where(upper, high, low)
    theirs_ref[:n, :] = jnp.where(upper, low, high).astype(BF16)
    z = idx_ref[1]
    shifts = [0] + [-1 - k for k in range(NZ // 2)] + [1 + k for k in range(NZ // 2 - 1)]
    for shift, extra in zip(shifts, extras):
        owner = lax.rem(z + NZ + shift, NZ)
        theirs_ref[pl.ds(pl.multiple_of(n + few * owner, few), few), :] = extra


def ring_indices(position, me):
    z = lax.rem(position, NZ)
    half = NZ // 2
    idx = [(position >= NZ).astype(jnp.int32), z]
    for distance in range(half, -1, -1):
        owners = [
            h * NZ + lax.rem(z + NZ + sign * distance, NZ) for sign in (1, -1) for h in range(NH)
        ]
        idx += [owner_slot(me, owner) for owner in owners] + owners
    return jnp.stack([i.astype(jnp.int32) for i in idx])


class Ring:
    def __init__(self, idx, by_slot, by_owner, extra, position):
        self.idx, self.position = idx, position
        self.arrays = [(x, 0) for x in by_slot] + [(x, 4) for x in by_owner]
        self.n = self.arrays[0][0].shape[1]
        self.columns = sum(x.shape[2] for x, _ in self.arrays)
        self.extras = [] if extra is None else [extra]
        self.few = sum(x.shape[0] for x in self.extras)
        self.rights, self.lefts = [], []

    def blocks(self, step, number):
        def place(which):
            return lambda i, idx: (idx[2 + 8 * step + which], 0, 0)

        specs, args = [], []
        for k in range(number):
            for x, base in self.arrays:
                specs.append(pl.BlockSpec((1,) + x.shape[1:], place(base + k)))
                args.append(x)
        return specs, args

    def run(self, kernel, after, specs, args, out_shape, scratch=()):
        def body(idx_ref, _, *refs):
            kernel(len(self.arrays), idx_ref, *refs)

        return pl.pallas_call(
            body,
            grid_spec=pltpu.PrefetchScalarGridSpec(
                num_scalar_prefetch=1,
                grid=(1,),
                in_specs=[pl.BlockSpec(memory_space=pl.ANY)] + specs,
                out_specs=[VMEM] * len(out_shape),
                scratch_shapes=list(scratch),
            ),
            out_shape=[jax.ShapeDtypeStruct(*o) for o in out_shape],
            compiler_params=pltpu.CompilerParams(vmem_limit_bytes=16 * 1024 * 1024),
            cost_estimate=pl.CostEstimate(flops=5 << 30, bytes_accessed=2 << 20, transcendentals=0),
        )(self.idx, after, *args)

    def send(self):
        self.r = tm_permute(self.r, lambda h, z: (h, (z + 1) % NZ))
        self.l = tm_permute(self.l, lambda h, z: (h, (z - 1) % NZ))

    def first(self, after):
        specs, args = self.blocks(0, 2)
        self.r, self.l = self.run(
            ring_first_kernel,
            after,
            specs + [VMEM] * len(self.extras),
            args + self.extras,
            [((self.n + self.few, self.columns), BF16)] * 2,
        )

    def step(self, step, after):
        specs, args = self.blocks(step, 4)

        def kernel(count, *refs):
            ring_step_kernel(count, step == 1, *refs)

        few = [((self.few, self.columns), BF16)] * 2 if self.few else []
        self.r, self.l, *passed = self.run(
            kernel,
            after,
            [VMEM] * 2 + specs,
            [self.r, self.l] + args,
            [((2 * self.n + self.few, self.columns), BF16)] * 2 + few,
        )
        self.rights += passed[:1]
        self.lefts += passed[1:]

    def last(self, after):
        few, columns = self.few, self.columns
        specs, args = self.blocks(NZ // 2, 2)
        passed = self.rights + self.lefts
        self.mine, self.r = self.run(
            ring_last_kernel,
            after,
            [VMEM] * 2 + specs + [VMEM] * len(self.extras + passed),
            [self.r, self.l] + args + self.extras + passed,
            [((self.n, columns), F32), ((self.n + NZ * few, columns), BF16)],
            [pltpu.VMEM((2 * self.n, columns), F32)],
        )

    def exchange(self):
        return tm_permute(self.r, lambda h, z: (h ^ 1, z))

    def finish(self, other):
        upper = self.position >= NZ
        total = self.mine + other[: self.n].astype(F32)
        if not self.few:
            return total, None
        theirs, other = self.r[self.n :], other[self.n :]
        gathered = [jnp.where(upper, other, theirs), jnp.where(upper, theirs, other)]
        return total, jnp.concatenate(gathered, 0)


def scatter_over_tm(one, two, beside, late):
    half = NZ // 2
    one.first(one.idx)
    two.first(one.r)
    for step in range(1, half + 1):
        before = two.r
        one.send()
        two.send()
        if step < half:
            one.step(step, before)
            two.step(step, one.r)
        else:
            one.last(before)
            two.last(one.r)
    others = one.exchange(), two.exchange()
    others, result = lax.optimization_barrier((others, late(beside)))
    return one.finish(others[0]), two.finish(others[1]), result


def forward_kernel(pair, q_ref, ka_ref, kb_ref, va_ref, vb_ref, *rest):
    if pair:
        last_ref, first_ref, w_ref, own_ref, o_ref, t_ref, p_ref, mean_ref, part_ref = rest
    else:
        o_ref, t_ref, p_ref = rest
    span = PATCHES
    step = 256
    k_rows = jnp.concatenate([ka_ref[...], kb_ref[...]], 1).T
    v_cols = jnp.concatenate([va_ref[...], vb_ref[...]], 1)
    for at in range(0, span, step):
        s = dot(k_rows, q_ref[:, at : at + step], 1, 0) * (HD ** (-0.5) * LOG2E)
        if pair:
            key = lax.broadcasted_iota(jnp.int32, s.shape, 0)
            s = jnp.where((key >= span) & (last_ref[0] == 1), -1e30, s)
        e = jnp.exp2(s - jnp.max(s, axis=0, keepdims=True))
        p = (e * (1.0 / jnp.sum(e, axis=0, keepdims=True))).astype(BF16)
        p_ref[:, at : at + step] = p
        o = dot(v_cols, p, 1, 0)
        o_ref[:, at : at + step] = o.astype(BF16)
        t_ref[at : at + step, :] = o.T.astype(BF16)
    if pair:
        row = lax.broadcasted_iota(jnp.int32, (16, span), 0)
        one = (jnp.where(row == 0, 1.0, 0.0) / span).astype(BF16)
        two = (jnp.where(row == 1, 1.0, 0.0) / span).astype(BF16)
        mean = dot(one, first_ref[...], 1, 1) + dot(two, o_ref[...], 1, 1)
        mean_ref[...] = mean[:2]
        part = split_dot(mean, w_ref[...], 1, 0)[:2] + own_ref[...]
        width = part_ref.shape[1]
        for i in range(4):
            part_ref[2 * i : 2 * i + 2, :] = part[:, i * width : (i + 1) * width]


def heads_kernel(
    bins_ref,
    flags_ref,
    last_ref,
    one_ref,
    two_ref,
    head_ref,
    w_ref,
    loss_ref,
    logit_ref,
    pooled_grad_ref,
    pooled_ref,
    shift_ref,
    scratch,
):
    scratch[...] = jnp.zeros_like(scratch)
    total = one_ref[...] + two_ref[...]
    part_width = total.shape[1]
    for i in range(4):
        scratch[0:2, i * part_width : (i + 1) * part_width] = total[2 * i : 2 * i + 2]
    pooled = scratch[...]
    pooled_ref[...] = pooled[:2]
    width = pooled.shape[1]
    scale = lax.rsqrt(jnp.sum(pooled * pooled, axis=1, keepdims=True) / width + 1e-05)
    logits = scale * split_dot(pooled, head_ref[...], 1, 0)
    rows = lax.broadcasted_iota(jnp.int32, (16, 1), 0)
    col = lax.broadcasted_iota(jnp.int32, logits.shape, 1)
    bins = logits.shape[1] - 1

    def pick(ref):
        return jnp.where(rows == 0, ref[0], ref[1])

    flags = pick(flags_ref)
    live = (rows < 2) & (flags != 2) & ((rows != 1) | (last_ref[0] == 0))
    live = jnp.where(live, 1.0, 0.0)
    target = jnp.where(flags == 1, 1.0, 0.0)
    is_bin = col < bins
    onehot = jnp.where(col == pick(bins_ref), 1.0, 0.0)
    top = jnp.max(jnp.where(is_bin, logits, -1e30), axis=1, keepdims=True)
    e = jnp.where(is_bin, jnp.exp(logits - top), 0.0)
    e_sum = jnp.sum(e, axis=1, keepdims=True)
    reward_loss = live * (jnp.log(e_sum) + top - jnp.sum(onehot * logits, axis=1, keepdims=True))
    term = jnp.sum(jnp.where(is_bin, 0.0, logits), axis=1, keepdims=True)
    small = jnp.exp(-jnp.abs(term))
    term_loss = live * (jnp.maximum(term, 0.0) + jnp.log1p(small) - target * term)
    sigmoid = jnp.where(term >= 0.0, 1.0, small) / (1.0 + small)
    grad = live * jnp.where(is_bin, e / e_sum - onehot, sigmoid - target)
    lane = lax.broadcasted_iota(jnp.int32, (16, 128), 1)
    loss_ref[...] = jnp.where(lane == 0, reward_loss, term_loss)[:8]
    scale_grad = jnp.sum(grad * logits, axis=1, keepdims=True) / scale
    through = scale * split_dot(grad, head_ref[...], 1, 1)
    pooled_grad = through - scale_grad * scale**3 * pooled / width
    logit_ref[...] = (scale * grad)[:2]
    pooled_grad_ref[...] = pooled_grad[:2]
    shift = pooled_grad / PATCHES
    high = shift.astype(BF16)
    low = (shift - high.astype(F32)).astype(BF16)
    shift_ref[...] = dot(w_ref[...], high, 1, 1) + dot(w_ref[...], low, 1, 1)


def backward_kernel(pair, q_ref, ka_ref, kb_ref, va_ref, vb_ref, p_ref, g_ref, shift_ref, *rest):
    if pair:
        dq_ref, da_ref, db_ref = rest
    else:
        add_ref, dq_ref, da_ref, db_ref = rest
    span = PATCHES
    step = 256
    k_cols = jnp.concatenate([ka_ref[...], kb_ref[...]], 1)
    v_rows = jnp.concatenate([va_ref[...], vb_ref[...]], 1).T
    lane = lax.broadcasted_iota(jnp.int32, shift_ref.shape, 1)
    shift = jnp.sum(jnp.where(lane == pair, shift_ref[...], 0.0), axis=1, keepdims=True)
    dk = jnp.zeros((HD, 2 * span), F32)
    dv = jnp.zeros((HD, 2 * span), F32)
    for at in range(0, span, step):
        first = pair * span + at
        g = (g_ref[:, first : first + step] + shift).astype(BF16)
        p_low = p_ref[:, at : at + step]
        p = p_low.astype(F32)
        dp = dot(v_rows, g, 1, 0)
        dv = dv + dot(g, p_low, 1, 1)
        delta = jnp.sum(p * dp, axis=0, keepdims=True)
        ds = (p * (dp - delta) * HD ** (-0.5)).astype(BF16)
        dq_ref[at : at + step, :] = dot(k_cols, ds, 1, 0).T.astype(BF16)
        dk = dk + dot(q_ref[:, at : at + step], ds, 1, 1)
    first = jnp.concatenate([dk[:, :span].T, dv[:, :span].T], 1)
    second = jnp.concatenate([dk[:, span:].T, dv[:, span:].T], 1)
    da_ref[...] = first
    if pair:
        db_ref[...] = second.astype(BF16)
    else:
        db_ref[...] = (second + add_ref[...]).astype(BF16)


def og_kernel(og_ref, w_ref, pooled_grad_ref, t0_ref, t1_ref, mean_ref, g_ref, out_ref):
    span = PATCHES

    @pl.when(pl.program_id(0) == 0)
    def _():
        g_ref[...] = jnp.zeros_like(g_ref)

    total = dot(og_ref[:, :span], t0_ref[...], 1, 0) + dot(og_ref[:, span:], t1_ref[...], 1, 0)
    row = pooled_grad_ref[...]
    column = jnp.concatenate([row, jnp.zeros((6, row.shape[1]), F32)], 0).T
    for pair in range(2):
        total = total + column[:, pair : pair + 1] * mean_ref[pair : pair + 1, :]
    out_ref[...] = total.astype(BF16)
    g_ref[...] += dot(w_ref[...], og_ref[...], 1, 0)


def order_kernel(owners_ref, q_ref, k_ref, v_ref, near_ref, far_ref, scratch):
    n = q_ref.shape[0] // 16
    for piece, out_ref in enumerate((near_ref, far_ref)):
        for i in range(8):
            first = pl.multiple_of(owners_ref[8 * piece + i] * n, n)
            for j, ref in enumerate((q_ref, k_ref, v_ref)):
                scratch[i * n : (i + 1) * n, j * HD : (j + 1) * HD] = ref[pl.ds(first, n), :]
        out_ref[...] = scratch[...].T


def near_kernel(*refs):
    *x_refs, w_ref, all_ref, out_ref = refs
    n = x_refs[0].shape[0]
    for i, ref in enumerate(x_refs):
        all_ref[i * n : (i + 1) * n, :] = ref[...]
    for at in range(0, 2 * PATCHES, PATCHES):
        out_ref[:, at : at + PATCHES] = dot(w_ref[...], all_ref[:, at : at + PATCHES], 1, 0)


def far_kernel(*refs):
    *x_refs, w_ref, near_ref, _, _, _, _, all_ref, kv0_ref, q0_ref, qkv1_ref = refs
    n = x_refs[0].shape[0]
    for i, ref in enumerate(x_refs):
        all_ref[i * n : (i + 1) * n, :] = ref[...]
    span = PATCHES
    first = near_ref[:, :span] + dot(w_ref[...], all_ref[:, :span], 1, 0)
    q0_ref[...] = first[:HD].astype(BF16)
    kv0_ref[...] = first[HD:].astype(BF16)
    second = near_ref[:, span:] + dot(w_ref[...], all_ref[:, span:], 1, 0)
    qkv1_ref[...] = second.astype(BF16)


def call(kernel, out_shape, specs, scratch=(), flops=0, bytes_accessed=0):
    return pl.pallas_call(
        kernel,
        out_shape=[jax.ShapeDtypeStruct(*o) for o in out_shape],
        in_specs=specs,
        out_specs=[VMEM] * len(out_shape),
        scratch_shapes=list(scratch),
        compiler_params=pltpu.CompilerParams(vmem_limit_bytes=24 * 1024 * 1024),
        cost_estimate=pl.CostEstimate(flops=flops, bytes_accessed=bytes_accessed, transcendentals=0),
    )


def local(
    frames,
    w_query,
    w_key,
    w_value,
    w_out,
    head_gain,
    reward_weight,
    term_weight,
    out_grad,
    reward_bins,
    episode_flags,
):
    rows, local_width = frames.shape
    span = PATCHES
    full_width = w_out.shape[1]
    n_tensor = lax.axis_size("tensor")
    position = lax.axis_index("tm")
    me = lax.axis_index("tensor")
    is_last = (position == lax.axis_size("tm") - 1).astype(jnp.int32).reshape(1)
    bins = reward_weight.shape[1]

    def gather(x):
        return lax.all_gather(x, "tensor", axis=0, tiled=True)

    head_local = jnp.concatenate([reward_weight, term_weight[:, None]], 1)
    head_sent = (head_gain[:, None] * head_local).astype(BF16)
    frames_t, head_sent = lax.optimization_barrier((frames.T, head_sent))
    head_full = gather(head_sent)
    frame_mean = frames.astype(F32).reshape(2, span, local_width).mean(axis=1)
    frame_mean = lax.dynamic_update_slice_in_dim(
        jnp.zeros((2, full_width), F32), frame_mean, me * local_width, 1
    )
    owners = [slot_owner(me, s) for s in range(n_tensor)]
    eight = n_tensor // 2 * local_width
    w_pieces = call(
        order_kernel,
        [((3 * HD, eight), BF16)] * 2,
        [SMEM] + [VMEM] * 3,
        [pltpu.VMEM((eight, 3 * HD), BF16)],
        bytes_accessed=5 << 20,
    )(jnp.stack(owners).astype(jnp.int32), w_query, w_key, w_value)
    grad_t = out_grad.T
    w_send = w_out.T.reshape(n_tensor, local_width, HD)

    project_flops = 2 * eight * 3 * HD * rows

    def project_near(near, beside):
        return call(
            near_kernel,
            [((eight, rows), BF16), ((3 * HD, rows), F32)],
            [VMEM] * 9,
            flops=project_flops,
            bytes_accessed=12 << 20,
        )(*near, beside[1][0])

    far, (frame_mean, w_pieces, grad_t, w_send), (x_near, qkv_near) = gather_hierarchical(
        frames_t, (frame_mean, w_pieces, grad_t, w_send), project_near
    )
    corners = tuple(x[:16, :HD] for x in far[:4])
    grad_t, head_full, corners = lax.optimization_barrier((grad_t, head_full, corners))
    og = gather(grad_t)
    x_far, kv0, q0, qkv1 = call(
        far_kernel,
        [
            ((eight, rows), BF16),
            ((2 * HD, span), BF16),
            ((HD, span), BF16),
            ((3 * HD, span), BF16),
        ],
        [VMEM] * 14,
        flops=project_flops,
        bytes_accessed=12 << 20,
    )(*far, w_pieces[1], qkv_near, *corners)
    kv_next = from_behind(kv0, -1)
    q1, kv1 = qkv1[:HD], qkv1[HD:]
    attention_flops = 2 * 2 * span * 2 * span * HD
    o_shape = ((HD, span), BF16)
    t_shape = ((span, HD), BF16)
    p_shape = ((2 * span, span), BF16)
    o0, t0, p0 = call(
        functools.partial(forward_kernel, 0),
        [o_shape, t_shape, p_shape],
        [VMEM] * 5,
        flops=attention_flops,
        bytes_accessed=3 << 20,
    )(q0, kv0[:HD], kv1[:HD], kv0[HD:], kv1[HD:])
    o1, t1, p1, att_mean, part = call(
        functools.partial(forward_kernel, 1),
        [o_shape, t_shape, p_shape, ((2, HD), F32), ((8, full_width // 4), F32)],
        [VMEM] * 5 + [SMEM, VMEM, VMEM, VMEM],
        flops=attention_flops,
        bytes_accessed=3 << 20,
    )(q1, kv1[:HD], kv_next[:HD], kv1[HD:], kv_next[HD:], is_last, o0, w_out, frame_mean)
    att = jnp.concatenate([o0, o1], 1)
    pooled_sum = sum_over_tensor(part)
    loss, logit_grad, pooled_grad, pooled, shift = call(
        heads_kernel,
        [
            ((8, 128), F32),
            ((2, bins + 1), F32),
            ((2, full_width), F32),
            ((2, full_width), F32),
            ((HD, 16), F32),
        ],
        [SMEM] * 3 + [VMEM] * 4,
        [pltpu.VMEM((16, full_width), F32)],
        flops=1 << 24,
        bytes_accessed=3 << 20,
    )(reward_bins, episode_flags, is_last, *pooled_sum, head_full, w_out)
    pair_losses = loss[:2, :2].T

    def mine(a):
        return lax.dynamic_slice_in_dim(a, me * local_width, local_width, 1)

    att_sent, og, shift = lax.optimization_barrier((att, og, shift))
    att_full = gather(att_sent)
    step_rows = 4 * local_width
    g, grad_t_out = pl.pallas_call(
        og_kernel,
        grid=(full_width // step_rows,),
        in_specs=[
            pl.BlockSpec((step_rows, rows), lambda i: (i, 0)),
            pl.BlockSpec((HD, step_rows), lambda i: (0, i)),
            pl.BlockSpec((2, step_rows), lambda i: (0, i)),
            pl.BlockSpec((span, HD), lambda i: (0, 0)),
            pl.BlockSpec((span, HD), lambda i: (0, 0)),
            pl.BlockSpec((2, HD), lambda i: (0, 0)),
        ],
        out_specs=[
            pl.BlockSpec((HD, rows), lambda i: (0, 0)),
            pl.BlockSpec((step_rows, HD), lambda i: (i, 0)),
        ],
        out_shape=[
            jax.ShapeDtypeStruct((HD, rows), F32),
            jax.ShapeDtypeStruct((full_width, HD), BF16),
        ],
        compiler_params=pltpu.CompilerParams(vmem_limit_bytes=48 * 1024 * 1024),
        cost_estimate=pl.CostEstimate(flops=4 << 30, bytes_accessed=8 << 20, transcendentals=0),
    )(og, w_out, pooled_grad, t0, t1, att_mean)

    def backward(pair, q, ka, kb, va, vb, p, g, *add):
        return call(
            functools.partial(backward_kernel, pair),
            [t_shape, ((span, 2 * HD), F32), ((span, 2 * HD), BF16)],
            [VMEM] * (8 + len(add)),
        )(q, ka, kb, va, vb, p, g, shift, *add)

    dq1, d_first1, d_next = backward(
        1, q1, kv1[:HD], kv_next[:HD], kv1[HD:], kv_next[HD:], p1, g
    )
    returned = from_behind(d_next, 1)
    dq0, d_first0, d1 = backward(
        0, q0, kv0[:HD], kv1[:HD], kv0[HD:], kv1[HD:], p0, g, d_first1
    )
    w_send, dq0, pooled, logit_grad = lax.optimization_barrier((w_send, dq0, pooled, logit_grad))
    w_cols = lax.all_to_all(w_send, "tensor", split_axis=0, concat_axis=0)
    d0 = (d_first0 + returned.astype(F32)).astype(BF16)
    d_all = jnp.concatenate(
        [jnp.concatenate([dq0, d0], 1), jnp.concatenate([dq1, d1], 1)], 0
    )

    def weight_grads(columns):
        parts = [dot(x, d_all[:, columns], 1, 0).astype(BF16) for x in (x_near, x_far)]
        return jnp.concatenate(parts, 0).reshape(n_tensor, local_width, -1)

    grad_t_qk, grad_t_v = weight_grads(slice(0, 2 * HD)), weight_grads(slice(2 * HD, 3 * HD))
    grad_t_out = grad_t_out.reshape(n_tensor, local_width, HD)

    pooled_mine = mine(pooled)
    gained = pooled_mine * head_gain[None, :]
    gain_in = jnp.dot(logit_grad, head_local.T, precision=lax.Precision.HIGHEST)
    gain_part = jnp.sum(pooled_mine * gain_in, axis=0, keepdims=True)
    small = jnp.concatenate([gained, gain_part], 0)
    small = jnp.pad(small, ((0, 0), (0, bins + 1 - local_width)))
    small = jnp.concatenate([small, logit_grad, jnp.zeros((3, bins + 1), F32)], 0)
    small_high = small.astype(BF16)
    small_low = (small - small_high.astype(F32)).astype(BF16)
    small = jnp.concatenate([small_high, small_low], 0)
    idx = ring_indices(position, me)
    def project_out(cols):
        cols = jnp.transpose(cols, (1, 0, 2)).reshape(local_width, n_tensor * HD)
        return (frames.astype(F32) + dot(att_full, cols, 0, 1)).astype(BF16)

    (qk, _), (vo, packed), mixed = scatter_over_tm(
        Ring(idx, [grad_t_qk], [], None, position),
        Ring(idx, [grad_t_v], [grad_t_out], small, position),
        w_cols,
        project_out,
    )
    packed = packed.astype(F32).reshape(-1, 2, 8, bins + 1)
    packed = packed[:, 0] + packed[:, 1]
    grad_query, grad_key = qk[:, :HD], qk[:, HD:]
    grad_value, grad_out = vo[:, :HD], vo[:, HD:].T
    gained_all = packed[:, :2, :local_width].reshape(-1, local_width)
    logit_all = packed[:, 3:5].reshape(-1, bins + 1)
    head_grad = lax.dot_general(
        gained_all,
        logit_all,
        (((0,), (0,)), ((), ())),
        precision=lax.Precision.HIGHEST,
        preferred_element_type=F32,
    )
    grad_gain = jnp.sum(packed[:, 2, :local_width], axis=0)
    return (
        mixed,
        pair_losses,
        grad_query,
        grad_key,
        grad_value,
        grad_out,
        head_grad[:, :bins],
        head_grad[:, bins],
        grad_gain,
    )


def solution(mesh):
    return jax.shard_map(
        local,
        mesh=mesh,
        in_specs=(
            P("tm", "tensor"),
            P(None, "tensor"),
            P(None, "tensor"),
            P(None, "tensor"),
            P("tensor", None),
            P("tensor"),
            P("tensor", None),
            P("tensor"),
            P("tm", "tensor"),
            P("tm"),
            P("tm"),
        ),
        out_specs=(
            P("tm", "tensor"),
            P(None, "tm"),
            P("tm", "tensor"),
            P("tm", "tensor"),
            P("tm", "tensor"),
            P("tensor", "tm"),
            P("tensor", None),
            P("tensor"),
            P("tensor"),
        ),
        check_vma=False,
    )
```
